768 devices in a mesh: slab: 16 (over y, core), dom: 48 (over x, z).
Axes of the slice: x: 4, y: 8, z: 12, core: 2. Of those that a mesh axis runs over, the one named last changes fastest.
Arguments:
- resident_now: bfloat16 [6144, 4096], P(('slab', 'dom')), may hold values from -6 to 6
- resident_old: bfloat16 [6144, 4096], P(('slab', 'dom')), may hold values from -6 to 6
- source_now: bfloat16 [73728, 4096], P(('slab', 'dom')), may hold values from -6 to 6
- source_old: bfloat16 [73728, 4096], P(('slab', 'dom')), may hold values from -6 to 6
- destination: int32 [73728], P(('slab', 'dom')), may hold values from -1 to 2303, as said below
- anchor: int32 [36864], P(('slab', 'dom')), may hold values from 0 to 47, as said below
- floor_height: int32 [43008, 256], P(('slab', 'dom')), may hold values from 0 to 7
- admit_class: int32 [43008], P(('slab', 'dom')), may hold values from 0 to 7
- admittance: float32 [8], replicated, may hold values from 0.05 to 1
- neighbours: int32 [6, 43008], P(None, ('slab', 'dom')), may hold values from -1 to 43007, as said below
Outputs:
- pressure: float32 [43008, 4096], P(('slab', 'dom'))
The draws below stay inside these ranges and needn't reach their ends.
Inputs may be any that keep to these rules, and one draw needn't show every extreme that they name: `destination`: each entry is -1 or o * 48 + j: the slot's brick becomes arriving brick j of dom index o in the same slab. Every arriving brick of every device comes from exactly one slot. The slots of one device send either none or exactly 2 bricks to each dom index. anchor agrees with destination: the named device of the same slab holds the slot whose destination is that arriving brick. Entry [f, b] is the global index of the brick across face f of brick b (faces -x, +x, -y, +y, -z, +z), or -1. If a meets c across face f, c meets a across the opposite face. -x and +x neighbours lie in the slab below and above (-1 at the first and last slab); -y and +y neighbours on another device of the same slab; -z and +z neighbours on the same device, and one of the two z faces of every brick is -1. For each face and each pair of devices at most 2 bricks of the first meet bricks of the second, and some pair reaches it.
All inputs are finite; a program needn't handle non-finite values.
Results may differ from the reference program's by a relative error of at most 0.0003.
Values may be sent and summed in bfloat16 or wider, within the bound.
No kernel may reach another device: no remote copies, remote signals or barrier semaphores. Data moves between devices by JAX's collectives and lax.ppermute only.
A program may use at most 64 MiB of HBM per device.

```python
import math
import jax
import jax.numpy as jnp
from jax import lax

EDGE = 16
CELLS = 4096
FACE = 256
RES = 8
CAP = 2
SETS = 24
MOVED = 48
OWN = 56
SRC = 96
FSET = 2
ITERS = 4
CLASSES = 8
BRICKS = 43008
KEPT = 6144
SLOTS = 73728
N_SLAB = 16
N_DOM = 48


def move_plan(key):

    def one_slab(slab_key):
        bias_key, noise_key, seat_key, spot_key = jax.random.split(slab_key, 4)
        bias = jax.random.randint(bias_key, (N_DOM,), 0, 3 * 32768)
        noise = jax.random.randint(noise_key, (N_DOM, N_DOM), 0, 65536)
        score = (noise + bias[None, :]) * N_DOM + jnp.arange(N_DOM, dtype=jnp.int32)[None, :]
        _, chosen = lax.top_k(score, SETS)
        chosen = chosen.astype(jnp.int32)
        seats = jax.vmap(lambda subkey: jax.random.permutation(subkey, MOVED))(jax.random.split(seat_key, N_DOM)).astype(jnp.int32)
        spots = jax.vmap(lambda subkey: jax.random.permutation(subkey, SRC))(jax.random.split(spot_key, N_DOM)).astype(jnp.int32)
        owner_ids = jnp.broadcast_to(jnp.arange(N_DOM, dtype=jnp.int32)[:, None, None], (N_DOM, SETS, CAP))
        within = jnp.broadcast_to(jnp.arange(CAP, dtype=jnp.int32)[None, None, :], (N_DOM, SETS, CAP))
        virtual = jnp.arange(SETS, dtype=jnp.int32)[:, None] * CAP + jnp.arange(CAP, dtype=jnp.int32)[None, :]
        seat = seats[:, virtual]
        sender = jnp.broadcast_to(chosen[:, :, None], (N_DOM, SETS, CAP))
        spot = spots[sender, owner_ids * CAP + within]
        arriving = owner_ids * MOVED + seat
        dest = jnp.full((N_DOM * SRC,), -1, jnp.int32).at[(sender * SRC + spot).reshape(-1)].set(arriving.reshape(-1))
        whence = jnp.zeros((N_DOM * MOVED,), jnp.int32).at[arriving.reshape(-1)].set(sender.reshape(-1))
        return (dest, whence)
    dest, whence = jax.vmap(one_slab)(jax.random.split(key, N_SLAB))
    return (dest.reshape(-1), whence.reshape(-1))


def draw_destination(key, part):
    return move_plan(key)[0]


def draw_anchor(key, part):
    return move_plan(key)[1]


def draw_neighbours(key, part):
    key = jax.random.fold_in(key, 7)
    seat_key, y_key, x_key = jax.random.split(key, 3)
    seats = jax.vmap(lambda subkey: jax.random.permutation(subkey, OWN))(jax.random.split(seat_key, N_SLAB * N_DOM))
    seats = seats.astype(jnp.int32).reshape(N_SLAB, N_DOM, OWN)
    y_shift = 1 + jax.vmap(lambda subkey: jax.random.permutation(subkey, N_DOM - 1))(jax.random.split(y_key, N_SLAB)).astype(jnp.int32)
    x_shift = jax.vmap(lambda subkey: jax.random.permutation(subkey, N_DOM))(jax.random.split(x_key, N_SLAB)).astype(jnp.int32)
    grid = (N_SLAB, N_DOM, OWN)
    slab_ids = jnp.broadcast_to(jnp.arange(N_SLAB, dtype=jnp.int32)[:, None, None], grid)
    dom_ids = jnp.broadcast_to(jnp.arange(N_DOM, dtype=jnp.int32)[None, :, None], grid)
    virtual = jnp.broadcast_to(jnp.arange(OWN, dtype=jnp.int32)[None, None, :], grid)
    run_ids = virtual // FSET
    y_off = y_shift[slab_ids, run_ids % (N_DOM - 1)]
    below_slab = jnp.maximum(slab_ids - 1, 0)
    above_slab = jnp.minimum(slab_ids + 1, N_SLAB - 1)
    x_here = x_shift[slab_ids, run_ids % N_DOM]
    x_below = x_shift[below_slab, run_ids % N_DOM]

    def locate(slab_at, dom_at, virtual_at):
        return (slab_at * N_DOM + dom_at) * OWN + seats[slab_at, dom_at, virtual_at]
    minus_x = jnp.where(slab_ids > 0, locate(below_slab, (dom_ids - x_below) % N_DOM, virtual), -1)
    plus_x = jnp.where(slab_ids < N_SLAB - 1, locate(above_slab, (dom_ids + x_here) % N_DOM, virtual), -1)
    minus_y = locate(slab_ids, (dom_ids - y_off) % N_DOM, virtual)
    plus_y = locate(slab_ids, (dom_ids + y_off) % N_DOM, virtual)
    odd_seat = virtual % 2 == 1
    minus_z = jnp.where(odd_seat, locate(slab_ids, dom_ids, jnp.maximum(virtual - 1, 0)), -1)
    plus_z = jnp.where(odd_seat, -1, locate(slab_ids, dom_ids, jnp.minimum(virtual + 1, OWN - 1)))
    links_all = jnp.stack([minus_x, plus_x, minus_y, plus_y, minus_z, plus_z]).reshape(6, -1).astype(jnp.int32)
    where_to = locate(slab_ids, dom_ids, virtual).reshape(-1)
    return jnp.full((6, BRICKS), -1, jnp.int32).at[:, where_to].set(links_all)


def plant(entries, stream_key, low, largest):
    longest = entries.shape.index(max(entries.shape))
    spots = []
    for shift in (0, 1):
        where = [jax.random.randint(jax.random.fold_in(stream_key, axis), (), 0, length) for axis, length in enumerate(entries.shape)]
        where[longest] = (where[longest] + shift) % entries.shape[longest]
        spots.append(tuple(where))
    return entries.at[spots[0]].set(low).at[spots[1]].set(largest)


def block_levels(rng, dims, cuts, smallest, largest):
    def one(position, shards_of):
        steps = jax.random.uniform(jax.random.fold_in(jax.random.fold_in(rng, 6), position), (shards_of,), jnp.float32, smallest / len(cuts), largest / len(cuts))
        return jnp.repeat(jnp.exp(steps), dims[position] // shards_of).reshape((-1,) + (1,) * (len(dims) - position - 1))

    loudness = one(*cuts[0])
    for cut in cuts[1:]:
        loudness = loudness * one(*cut)
    return loudness


def centred(key, dims, spread, reach, cuts=(), held_as=jnp.bfloat16):
    loudness = block_levels(key, dims, cuts, -0.22, 0.18) if cuts else 1.0
    array = jax.random.normal(key, dims, jnp.float32) * spread * loudness
    return jnp.minimum(jnp.maximum(array, -reach), reach).astype(held_as)


def setup_inputs(seed: int = 0) -> dict:
    keys = jax.random.split(jax.random.key(seed), 11)
    resident_now = centred(keys[0], (KEPT, CELLS), 1.0, 6.0, ((0, 768),))
    resident_old = centred(keys[1], (KEPT, CELLS), 1.0, 6.0, ((0, 768),))
    source_now = centred(keys[2], (SLOTS, CELLS), 1.0, 6.0, ((0, 768),))
    source_old = centred(keys[3], (SLOTS, CELLS), 1.0, 6.0, ((0, 768),))
    destination = draw_destination(jax.random.fold_in(keys[10], 71), 0)
    anchor = draw_anchor(jax.random.fold_in(keys[10], 71), 0)
    floor_height = plant(jax.random.randint(keys[6], (BRICKS, FACE), 0, EDGE // 2), jax.random.fold_in(keys[6], 1), 0, (EDGE // 2) - 1).astype(jnp.int32)
    admit_class = plant(jax.random.randint(keys[7], (BRICKS,), 0, CLASSES), jax.random.fold_in(keys[7], 1), 0, CLASSES - 1).astype(jnp.int32)
    admittance = jnp.clip(jnp.exp(jax.random.uniform(keys[8], (CLASSES,), jnp.float32, math.log(0.05), math.log(1.0))), 0.05, 1.0)
    neighbours = draw_neighbours(jax.random.fold_in(keys[10], 71), 0)
    return dict(resident_now=resident_now, resident_old=resident_old, source_now=source_now, source_old=source_old, destination=destination, anchor=anchor, floor_height=floor_height, admit_class=admit_class, admittance=admittance, neighbours=neighbours)


courant_sq = 0.3
courant = 0.3 ** 0.5


def face_layers(volume):
    number, cell_len = volume.shape[0], volume.shape[1]
    face_len = EDGE * EDGE
    planes = volume.reshape(number, EDGE, face_len)
    return [volume[:, :face_len], volume[:, cell_len - face_len:],
            planes[:, :, :EDGE].reshape(number, -1), planes[:, :, face_len - EDGE:].reshape(number, -1),
            volume[:, 0::EDGE], volume[:, EDGE - 1::EDGE]]


def neighbour_sum(volume, ghosts):
    number, cell_len = volume.shape[0], volume.shape[1]
    face_len = EDGE * EDGE
    below_x = jnp.concatenate([ghosts[0], volume[:, :-face_len]], axis=1)
    above_x = jnp.concatenate([volume[:, face_len:], ghosts[1]], axis=1)
    planes = volume.reshape(number, EDGE, face_len)
    below_y = jnp.concatenate([ghosts[2].reshape(number, EDGE, EDGE), planes[:, :, :-EDGE]], axis=2).reshape(number, cell_len)
    above_y = jnp.concatenate([planes[:, :, EDGE:], ghosts[3].reshape(number, EDGE, EDGE)], axis=2).reshape(number, cell_len)
    depth = jnp.arange(cell_len, dtype=jnp.int32) % EDGE
    blank = jnp.zeros((number, 1), volume.dtype)
    below_z = jnp.where(depth[None, :] == 0, jnp.repeat(ghosts[4], EDGE, axis=1), jnp.concatenate([blank, volume[:, :-1]], axis=1))
    above_z = jnp.where(depth[None, :] == EDGE - 1, jnp.repeat(ghosts[5], EDGE, axis=1), jnp.concatenate([volume[:, 1:], blank], axis=1))
    return below_x + above_x + below_y + above_y + below_z + above_z


def air_cells(heights):
    cell_len = heights.shape[1] * EDGE
    levels = jnp.arange(cell_len, dtype=jnp.int32) % EDGE
    return (levels[None, :] >= jnp.repeat(heights, EDGE, axis=1)).astype(jnp.float32)


def count_open(air_mask, present, below_air, above_air):
    number = air_mask.shape[0]
    flat_len = EDGE * EDGE
    ghosts = [jnp.broadcast_to(present[direction][:, None], (number, flat_len)).astype(jnp.float32) for direction in range(4)]
    return neighbour_sum(air_mask, ghosts + [below_air, above_air])


def leapfrog(current, lagging, air_mask, open_count, rates, ghosts):
    summed = neighbour_sum(current, ghosts)
    damping = courant * (6.0 - open_count) * rates[:, None] / 2.0
    return air_mask * (((2.0 - open_count * courant_sq) * current + courant_sq * summed - (1.0 - damping) * lagging) / (1.0 + damping))


def reference(resident_now, resident_old, source_now, source_old, destination, anchor, floor_height, admit_class, admittance, neighbours):
    groups = N_SLAB * N_DOM
    wanted = jnp.arange(N_DOM, dtype=jnp.int32)[:, None] * MOVED + jnp.arange(MOVED, dtype=jnp.int32)[None, :]
    slot_ids = jnp.arange(SRC, dtype=jnp.int32)

    def find_slots(inputs_pair):
        dest_slab, anchor_slab = inputs_pair
        rows_seen = dest_slab[anchor_slab]
        return jnp.sum(jnp.where(rows_seen == wanted[:, :, None], slot_ids, 0), axis=2).astype(jnp.int32)

    anchor_grid = anchor.reshape(N_SLAB, N_DOM, MOVED)
    found = lax.map(find_slots, (destination.reshape(N_SLAB, N_DOM, SRC), anchor_grid))
    slab_index = jnp.arange(N_SLAB, dtype=jnp.int32)[:, None, None]
    source_rows = ((slab_index * N_DOM + anchor_grid) * SRC + found).reshape(groups, MOVED).astype(jnp.int32)
    current = jnp.concatenate([resident_now.reshape(groups, RES, CELLS), source_now[source_rows]], axis=1)
    previous = jnp.concatenate([resident_old.reshape(groups, RES, CELLS), source_old[source_rows]], axis=1)

    heights = floor_height.reshape(groups, OWN, FACE)
    rates = admittance[admit_class].reshape(groups, OWN)
    links = neighbours.reshape(6, groups, OWN).transpose(1, 0, 2)
    air_bottom = (floor_height == 0).astype(jnp.float32)
    air_top = (floor_height <= EDGE - 1).astype(jnp.float32)

    def start(block_in):
        height_blk, now_blk, old_blk = block_in
        air_mask = air_cells(height_blk)
        return air_mask * now_blk.astype(jnp.float32), air_mask * old_blk.astype(jnp.float32)

    state, lagging = lax.map(start, (heights, current, previous))

    for sweep_no in range(ITERS):
        layers = face_layers(state.reshape(groups * OWN, CELLS))

        def advance(block_in):
            now_blk, old_blk, link_blk, height_blk, rate_blk = block_in
            air_mask = air_cells(height_blk)
            present = [link_blk[direction] >= 0 for direction in range(4)]
            below_air = jnp.where((link_blk[4] >= 0)[:, None], air_top[jnp.maximum(link_blk[4], 0)], 0.0)
            above_air = jnp.where((link_blk[5] >= 0)[:, None], air_bottom[jnp.maximum(link_blk[5], 0)], 0.0)
            open_count = count_open(air_mask, present, below_air, above_air)
            ghosts = []
            for direction in range(6):
                target = link_blk[direction]
                ghosts.append(jnp.where((target >= 0)[:, None], layers[direction ^ 1][jnp.maximum(target, 0)], 0.0))
            return leapfrog(now_blk, old_blk, air_mask, open_count, rate_blk, ghosts)

        updated_all = lax.map(advance, (state, lagging, links, heights, rates))
        lagging, state = state, updated_all
    return state.reshape(BRICKS, CELLS)
```

```python
import functools

import jax
import jax.numpy as jnp
from jax import lax
from jax.experimental import pallas as pl
from jax.experimental.pallas import tpu as pltpu
from jax.sharding import PartitionSpec as P

EDGE = 16
CAP = 2
ITERS = 4
FACE = EDGE * EDGE
CELLS = EDGE * FACE
LANES = 128
SUB = 8
DIRS = 4
ROWS = DIRS * CAP

courant_sq = 0.3
courant = 0.3**0.5

OCTAVE = 1024.0
LOWEST = 23.5

VMEM = pltpu.CompilerParams(vmem_limit_bytes=44 * 1024 * 1024)


def rank_within(groups, orderings, usable):
    earlier = (
        (groups[:, None] == groups[None, :])
        & (orderings[None, :] < orderings[:, None])
        & usable[None, :]
    )
    return jnp.sum(earlier.astype(jnp.int32), axis=1)


def encode(values):
    size = jnp.abs(values)
    level = jnp.floor((jnp.log2(jnp.maximum(size, 1e-30)) + LOWEST) * OCTAVE + 0.5)
    level = jnp.clip(level, 0.0, 32767.0)
    return jnp.where(values < 0.0, -level, level).astype(jnp.int32).astype(jnp.int16)


def decode(codes):
    level = codes.astype(jnp.int32).astype(jnp.float32)
    size = jnp.exp2(jnp.abs(level) * (1.0 / OCTAVE) - LOWEST)
    return jnp.where(level > 0.0, size, jnp.where(level < 0.0, -size, 0.0))


def halves(values):
    high = values.astype(jnp.bfloat16)
    low = (values - high.astype(jnp.float32)).astype(jnp.bfloat16)
    return high, low


def picked(matrix, values):
    high, low = halves(values)
    return jnp.dot(matrix, high, preferred_element_type=jnp.float32) + jnp.dot(
        matrix, low, preferred_element_type=jnp.float32
    )


def turn(block, shift, axis=1):
    size = block.shape[axis]
    shift = shift % size
    return pltpu.roll(block, shift, axis) if shift else block


class Grid:
    def __init__(self, joined):
        lane = lax.broadcasted_iota(jnp.int32, (SUB, LANES), 1)
        row = lax.broadcasted_iota(jnp.int32, (SUB, LANES), 0)
        self.first_y = lane < EDGE
        self.last_y = lane >= LANES - EDGE
        self.bottom = lane % EDGE == 0
        self.top = lane % EDGE == EDGE - 1
        self.odd = row % 2 == 1
        self.strip = lane // EDGE
        upper = jnp.where(self.odd, 1.0, 0.0)
        self.joined_down = joined * upper
        self.joined_up = joined * (1.0 - upper)

    def along_z(self, block):
        partner = jnp.where(self.odd, turn(block, 1, 0), turn(block, -1, 0))
        below = jnp.where(
            self.bottom, turn(partner, 1 - EDGE) * self.joined_down, turn(block, 1)
        )
        above = jnp.where(self.top, turn(partner, EDGE - 1) * self.joined_up, turn(block, -1))
        return below + above

    def total(self, plane, x, ghost_x, ghost_y):
        first, second = plane(x)
        before = plane(x - 1) if x else ghost_x(0)
        after = plane(x + 1) if x < EDGE - 1 else ghost_x(1)
        up_first, up_second = turn(first, EDGE), turn(second, EDGE)
        down_first, down_second = turn(first, -EDGE), turn(second, -EDGE)
        low, high = ghost_y(x)
        total_first = (
            (before[0] + after[0])
            + (jnp.where(self.first_y, low, up_first) + jnp.where(self.last_y, down_second, down_first))
            + self.along_z(first)
        )
        total_second = (
            (before[1] + after[1])
            + (jnp.where(self.first_y, up_first, up_second) + jnp.where(self.last_y, high, down_second))
            + self.along_z(second)
        )
        return total_first, total_second


def pieces(ref, rows, x):
    at = x * FACE
    return ref[rows, at : at + LANES], ref[rows, at + LANES : at + FACE]


class Faces:
    def __init__(self, ref, owned, grid):
        self.ref, self.owned, self.grid = ref, owned, grid
        self.low = [None, None]
        self.high = [None, None]

    def add(self, x, first, second, group):
        if x in (0, EDGE - 1):
            at = pl.ds(pl.multiple_of((self.owned if x else 0) + group * SUB, SUB), SUB)
            self.ref[at, :LANES] = first
            self.ref[at, LANES:] = second
        half, place = x // SUB, x % SUB
        here = self.grid.strip == place
        low = turn(first, EDGE * place)
        high = turn(second, EDGE * (place + 1))
        self.low[half] = low if place == 0 else jnp.where(here, low, self.low[half])
        self.high[half] = high if place == 0 else jnp.where(here, high, self.high[half])

    def finish(self, group):
        for order, parts in ((2, self.low), (3, self.high)):
            at = pl.ds(pl.multiple_of(order * self.owned + group * SUB, SUB), SUB)
            self.ref[at, :LANES] = parts[0]
            self.ref[at, LANES:] = parts[1]


def as_message(rows):
    number = rows.shape[0] // ROWS
    return jnp.concatenate(
        [rows[:, :LANES].reshape(number, ROWS, LANES), rows[:, LANES:].reshape(number, ROWS, LANES)],
        axis=1,
    )


def from_message(message):
    number = message.shape[0]
    return jnp.concatenate(
        [
            message[:, :ROWS].reshape(number * ROWS, LANES),
            message[:, ROWS:].reshape(number * ROWS, LANES),
        ],
        axis=1,
    )


def pack_kernel(incoming, members, dest_ref, now_ref, old_ref, out_ref):
    slots = dest_ref.shape[1]
    dest = dest_ref[...]
    src = lax.broadcasted_iota(jnp.int32, (slots, slots), 1)
    other = lax.broadcasted_iota(jnp.int32, (slots, slots), 0)
    across = jnp.broadcast_to(dest, (slots, slots))
    down = jnp.sum(jnp.where(src == other, across, 0), axis=1, keepdims=True)
    receiver = jnp.zeros((1, slots), jnp.int32)
    base = jnp.zeros((1, slots), jnp.int32)
    for member in range(1, members):
        reached = dest >= member * incoming
        receiver = receiver + reached.astype(jnp.int32)
    base = receiver * incoming
    earlier = (down >= base) & (down < dest)
    place = jnp.sum(earlier.astype(jnp.int32), axis=0, keepdims=True)
    spot = jnp.where(dest >= 0, receiver * CAP + place, -1)
    chosen = jnp.where(other == spot, 1.0, 0.0).astype(jnp.bfloat16)
    cells = now_ref.shape[1]
    for index, ref in ((0, now_ref), (1, old_ref)):
        rows = jnp.dot(chosen, ref[...], preferred_element_type=jnp.float32)
        out_ref[:, :, index * cells : (index + 1) * cells] = rows.astype(jnp.bfloat16).reshape(
            members, CAP, cells
        )


def prepare_kernel(height_ref, present_ref, rate_ref, mask_ref, keep_ref, gain_ref, lag_ref):
    owned = height_ref.shape[0]
    row = lax.broadcasted_iota(jnp.int32, (FACE, FACE), 0)
    column = lax.broadcasted_iota(jnp.int32, (FACE, FACE), 1)
    level = (lax.broadcasted_iota(jnp.int32, (owned, FACE), 1) % EDGE).astype(jnp.float32)
    heights = height_ref[...].astype(jnp.bfloat16)
    for x in range(EDGE):
        spread = jnp.where(row == column // EDGE + x * EDGE, 1.0, 0.0).astype(jnp.bfloat16)
        floor = jnp.dot(heights, spread, preferred_element_type=jnp.float32)
        mask_ref[:, x * FACE : (x + 1) * FACE] = jnp.where(level >= floor, 1.0, 0.0)

    def group_step(group, carry):
        rows = pl.ds(pl.multiple_of(group * SUB, SUB), SUB)
        present = present_ref[rows, :]
        near = [jnp.broadcast_to(present[:, d : d + 1], (SUB, LANES)) for d in range(6)]
        rate = jnp.broadcast_to(rate_ref[rows, :1], (SUB, LANES))
        grid = Grid(near[4] + near[5])
        for x in range(EDGE):
            count = grid.total(
                lambda at: pieces(mask_ref, rows, at),
                x,
                lambda d: (near[d], near[d]),
                lambda at: (near[2], near[3]),
            )
            air = pieces(mask_ref, rows, x)
            for half in range(2):
                damping = courant * (6.0 - count[half]) * rate / 2.0
                share = air[half] / (1.0 + damping)
                at = slice(x * FACE + half * LANES, x * FACE + (half + 1) * LANES)
                keep_ref[rows, at] = (2.0 - count[half] * courant_sq) * share
                gain_ref[rows, at] = courant_sq * share
                lag_ref[rows, at] = (1.0 - damping) * share
        return carry

    lax.fori_loop(0, owned // SUB, group_step, 0)


def begin_kernel(
    got_ref, now_ref, old_ref, chosen_ref, kept_ref, mask_ref, send_ref, p_ref, q_ref, out_ref, face_ref
):
    members, _, width = got_ref.shape
    owned, cells = p_ref.shape
    chosen = chosen_ref[...]
    kept = kept_ref[...]
    for index, (own_ref, to_ref) in enumerate(((now_ref, p_ref), (old_ref, q_ref))):
        arrived = got_ref[:, :, index * cells : (index + 1) * cells].reshape(members * CAP, cells)
        rows = jnp.dot(chosen, arrived, preferred_element_type=jnp.float32)
        rows = rows + jnp.dot(kept, own_ref[...], preferred_element_type=jnp.float32)
        to_ref[...] = mask_ref[...] * rows

    def group_step(group, carry):
        rows = pl.ds(pl.multiple_of(group * SUB, SUB), SUB)
        faces = Faces(face_ref, owned, Grid(jnp.ones((SUB, LANES), jnp.float32)))
        for x in range(EDGE):
            faces.add(x, *pieces(p_ref, rows, x), group)
        faces.finish(group)
        return carry

    lax.fori_loop(0, owned // SUB, group_step, 0)
    sent = jnp.dot(
        send_ref[...], face_ref[...].astype(jnp.bfloat16), preferred_element_type=jnp.float32
    )
    out_ref[...] = as_message(sent).astype(jnp.bfloat16)


def step_kernel(
    coded,
    last,
    here_ref,
    low_ref,
    high_ref,
    take_ref,
    send_ref,
    joined_ref,
    p_ref,
    q_ref,
    keep_ref,
    gain_ref,
    lag_ref,
    new_ref,
    out_ref,
    ghost_ref,
    face_ref,
):
    owned = p_ref.shape[0]
    for ref, low_row, number in ((low_ref, 0, 1), (high_ref, 1, 1), (here_ref, 2, 2)):
        at = slice(low_row * owned, (low_row + number) * owned)
        matrix = take_ref[at, :]
        if coded:
            ghost_ref[at, :] = picked(matrix, from_message(decode(ref[...])))
        else:
            received = from_message(ref[...].astype(jnp.float32)).astype(jnp.bfloat16)
            ghost_ref[at, :] = jnp.dot(matrix, received, preferred_element_type=jnp.float32)
    target_ref = face_ref if last else new_ref

    def group_step(group, carry):
        rows = pl.ds(pl.multiple_of(group * SUB, SUB), SUB)
        grid = Grid(jnp.broadcast_to(joined_ref[rows, :1], (SUB, LANES)))
        ghosts = []
        for d in range(DIRS):
            at = pl.ds(pl.multiple_of(d * owned + group * SUB, SUB), SUB)
            ghosts.append((ghost_ref[at, :LANES], ghost_ref[at, LANES:]))

        def ghost_y(x):
            half, place = x // SUB, x % SUB
            low = turn(ghosts[2][half], -EDGE * place)
            high = turn(ghosts[3][half], -EDGE * (place + 1))
            return low, high

        faces = None if last else Faces(face_ref, owned, grid)
        for x in range(EDGE):
            total = grid.total(
                lambda at: pieces(p_ref, rows, at), x, lambda d: ghosts[d], ghost_y
            )
            state = pieces(p_ref, rows, x)
            lagging = pieces(q_ref, rows, x)
            keep = pieces(keep_ref, rows, x)
            gain = pieces(gain_ref, rows, x)
            lag = pieces(lag_ref, rows, x)
            updated = [
                keep[h] * state[h] + gain[h] * total[h] - lag[h] * lagging[h] for h in range(2)
            ]
            for h in range(2):
                target_ref[rows, x * FACE + h * LANES : x * FACE + (h + 1) * LANES] = updated[h]
            if faces is not None:
                faces.add(x, updated[0], updated[1], group)
        if faces is not None:
            faces.finish(group)
        return carry

    lax.fori_loop(0, owned // SUB, group_step, 0)
    if last:
        new_ref[...] = picked(send_ref[...], face_ref[...])
    else:
        out_ref[...] = encode(as_message(picked(send_ref[...], face_ref[...])))


def last_kernel(*refs):
    ins, (new_ref, ghost_ref, state_ref) = refs[:-3], refs[-3:]
    step_kernel(True, True, *ins, new_ref, None, ghost_ref, state_ref)


def on_device(
    resident_now,
    resident_old,
    source_now,
    source_old,
    destination,
    anchor,
    floor_height,
    admit_class,
    admittance,
    neighbours,
):
    members = lax.axis_size("dom")
    slabs = lax.axis_size("slab")
    owned = floor_height.shape[0]
    incoming = anchor.shape[0]
    cells = source_now.shape[1]
    kept = owned - incoming
    f32, bf16, i32 = jnp.float32, jnp.bfloat16, jnp.int32

    outgoing = pl.pallas_call(
        functools.partial(pack_kernel, incoming, members),
        out_shape=jax.ShapeDtypeStruct((members, CAP, 2 * cells), bf16),
        compiler_params=VMEM,
    )(destination[None, :], source_now, source_old)
    got = lax.all_to_all(outgoing, "dom", split_axis=0, concat_axis=0, tiled=True)

    present = neighbours >= 0
    peer_dev = neighbours // owned % members
    peer_slot = neighbours % owned
    slot_ids = jnp.arange(owned, dtype=i32)
    lower = present[5]
    upper = present[4]
    lower_rank = jnp.sum((lower[None, :] & (slot_ids[None, :] < slot_ids[:, None])).astype(i32), axis=1)
    partner_rank = jnp.sum(
        (lower[None, :] & (slot_ids[None, :] < peer_slot[4][:, None])).astype(i32), axis=1
    )
    alone = ~(lower | upper)
    alone_rank = jnp.sum((alone[None, :] & (slot_ids[None, :] < slot_ids[:, None])).astype(i32), axis=1)
    pairs = jnp.sum(lower.astype(i32))
    position = jnp.where(
        lower, 2 * lower_rank, jnp.where(upper, 2 * partner_rank + 1, 2 * pairs + alone_rank)
    )
    order_is = position[None, :] == slot_ids[:, None]
    order = jnp.sum(jnp.where(order_is, slot_ids[None, :], 0), axis=1)
    back = (position[:, None] == slot_ids[None, :]).astype(bf16)

    seat = rank_within(anchor, jnp.arange(incoming, dtype=i32), anchor >= 0)
    inbox = jnp.concatenate([jnp.full((kept,), -1, i32), anchor * CAP + seat])
    class_ids = jnp.arange(admittance.shape[0], dtype=i32)
    send_at = []
    take_at = []
    for d in range(DIRS):
        order_out = rank_within(peer_dev[d], peer_slot[d], present[d])
        order_in = rank_within(peer_dev[d], slot_ids, present[d])
        send_at.append(jnp.where(present[d], peer_dev[d] * ROWS + d * CAP + order_out, -1))
        take_at.append(jnp.where(present[d], peer_dev[d] * ROWS + (d ^ 1) * CAP + order_in, -1))
    table = jnp.stack(
        send_at + take_at + [inbox, admit_class] + [present[d].astype(i32) for d in range(6)]
    )
    table = jnp.sum(jnp.where(order_is[None], table[:, None, :], 0), axis=2)
    message_rows = jnp.arange(members * ROWS, dtype=i32)
    send = (table[:DIRS].reshape(1, -1) == message_rows[:, None]).astype(bf16)
    take = (table[DIRS : 2 * DIRS].reshape(-1, 1) == message_rows[None, :]).astype(bf16)
    chosen = (table[8][:, None] == jnp.arange(members * CAP, dtype=i32)[None, :]).astype(bf16)
    stay = (order[:, None] == jnp.arange(kept, dtype=i32)[None, :]).astype(bf16)
    rates = jnp.sum(
        jnp.where(table[9][:, None] == class_ids[None, :], admittance[None, :], 0.0), axis=1
    )[:, None]
    near = table[10:].T.astype(f32)
    joined = near[:, 4:5] + near[:, 5:6]
    heights = floor_height[order].astype(f32)

    grid_shape = jax.ShapeDtypeStruct((owned, cells), f32)
    mask, keep, gain, lag = pl.pallas_call(
        prepare_kernel,
        out_shape=[grid_shape] * 4,
        compiler_params=VMEM,
    )(heights, near, rates)

    message = (members, 2 * ROWS, LANES)
    state, lagging, outbox = pl.pallas_call(
        begin_kernel,
        out_shape=[grid_shape, grid_shape, jax.ShapeDtypeStruct(message, bf16)],
        scratch_shapes=[pltpu.VMEM((DIRS * owned, FACE), f32)],
        compiler_params=VMEM,
    )(got, resident_now, resident_old, chosen, stay, mask, send)

    ends = slabs - 1
    for sweep in range(ITERS):
        here = lax.all_to_all(outbox, "dom", split_axis=0, concat_axis=0, tiled=True)
        from_low = lax.ppermute(here, "slab", [(i, i + 1) for i in range(ends)])
        from_high = lax.ppermute(here, "slab", [(i + 1, i) for i in range(ends)])
        common = (here, from_low, from_high, take)
        fields = (joined, state, lagging, keep, gain, lag)
        ghost_scratch = pltpu.VMEM((DIRS * owned, FACE), f32)
        if sweep < ITERS - 1:
            updated, outbox = pl.pallas_call(
                functools.partial(step_kernel, sweep > 0, False),
                out_shape=[grid_shape, jax.ShapeDtypeStruct(message, jnp.int16)],
                scratch_shapes=[ghost_scratch, pltpu.VMEM((DIRS * owned, FACE), f32)],
                compiler_params=VMEM,
            )(*common, send, *fields)
        else:
            updated = pl.pallas_call(
                last_kernel,
                out_shape=grid_shape,
                scratch_shapes=[ghost_scratch, pltpu.VMEM((owned, cells), f32)],
                compiler_params=VMEM,
            )(*common, back, *fields)
        lagging, state = state, updated
    return state


def solution(mesh):
    split = P(("slab", "dom"), None)
    line = P(("slab", "dom"))
    return jax.shard_map(
        on_device,
        mesh=mesh,
        in_specs=(split, split, split, split, line, line, split, line, P(), P(None, ("slab", "dom"))),
        out_specs=split,
        check_vma=False,
    )
```

```python
import functools

import jax
import jax.numpy as jnp
from jax import lax
from jax.experimental import pallas as pl
from jax.experimental.pallas import tpu as pltpu
from jax.sharding import PartitionSpec as P

EDGE = 16
CAP = 2
ITERS = 4
FACE = EDGE * EDGE
CELLS = EDGE * FACE
LANES = 128
SUB = 8
DIRS = 4
ROWS = DIRS * CAP
CHUNKS = 4

INBOX, ORDER, RATE, JOINED, NEAR = 0, 1, 2, 3, 4

courant_sq = 0.3
courant = 0.3**0.5

OCTAVE = 1024.0
LOWEST = 23.5

VMEM = pltpu.CompilerParams(vmem_limit_bytes=16 * 1024 * 1024)


def rank_within(groups, orderings, usable):
    earlier = (
        (groups[:, None] == groups[None, :])
        & (orderings[None, :] < orderings[:, None])
        & usable[None, :]
    )
    return jnp.sum(earlier.astype(jnp.int32), axis=1)


def encode(values):
    size = jnp.abs(values)
    level = jnp.floor((jnp.log2(jnp.maximum(size, 1e-30)) + LOWEST) * OCTAVE + 0.5)
    level = jnp.clip(level, 0.0, 32767.0)
    return jnp.where(values < 0.0, -level, level)


def decode(level):
    size = jnp.exp2(jnp.abs(level) * (1.0 / OCTAVE) - LOWEST)
    return jnp.where(level > 0.0, size, jnp.where(level < 0.0, -size, 0.0))


def picked(matrix, values):
    high = values.astype(jnp.bfloat16)
    low = (values - high.astype(jnp.float32)).astype(jnp.bfloat16)
    width = values.shape[1]
    if width == LANES:
        both = jnp.dot(
            matrix, jnp.concatenate([high, low], axis=1), preferred_element_type=jnp.float32
        )
        return both[:, :width] + both[:, width:]
    return jnp.dot(matrix, high, preferred_element_type=jnp.float32) + jnp.dot(
        matrix, low, preferred_element_type=jnp.float32
    )


def turn(block, shift, axis=1):
    size = block.shape[axis]
    shift = shift % size
    return pltpu.roll(block, shift, axis) if shift else block


class Grid:
    def __init__(self, joined):
        lane = lax.broadcasted_iota(jnp.int32, (SUB, LANES), 1)
        row = lax.broadcasted_iota(jnp.int32, (SUB, LANES), 0)
        self.first_y = lane < EDGE
        self.last_y = lane >= LANES - EDGE
        self.bottom = lane % EDGE == 0
        self.top = lane % EDGE == EDGE - 1
        self.odd = row % 2 == 1
        self.strip = lane // EDGE
        upper = jnp.where(self.odd, 1.0, 0.0)
        self.joined_down = joined * upper
        self.joined_up = joined * (1.0 - upper)

    def along_z(self, block):
        partner = jnp.where(self.odd, turn(block, 1, 0), turn(block, -1, 0))
        below = jnp.where(
            self.bottom, turn(partner, 1 - EDGE) * self.joined_down, turn(block, 1)
        )
        above = jnp.where(self.top, turn(partner, EDGE - 1) * self.joined_up, turn(block, -1))
        return below + above

    def total(self, plane, x, ghost_x, ghost_y):
        first, second = plane(x)
        sides = [plane(at) for at in (x - 1, x + 1) if 0 <= at < EDGE]
        if ghost_x is not None and x in (0, EDGE - 1):
            sides.append(ghost_x(x))
        along_x = [sum(side[half] for side in sides) for half in range(2)]
        up_first, up_second = turn(first, EDGE), turn(second, EDGE)
        down_first, down_second = turn(first, -EDGE), turn(second, -EDGE)
        low, high = ghost_y(x)
        total_first = (
            along_x[0]
            + (jnp.where(self.first_y, low, up_first) + jnp.where(self.last_y, down_second, down_first))
            + self.along_z(first)
        )
        total_second = (
            along_x[1]
            + (jnp.where(self.first_y, up_first, up_second) + jnp.where(self.last_y, high, down_second))
            + self.along_z(second)
        )
        return total_first, total_second


def pieces(ref, rows, x):
    at = x * FACE
    return ref[rows, at : at + LANES], ref[rows, at + LANES : at + FACE]


def plane(ref, ends_ref, rows, x):
    if x in (0, EDGE - 1):
        return pieces(ends_ref, rows, 1 if x else 0)
    return pieces(ref, rows, x)


def at_rows(base, group):
    return pl.ds(pl.multiple_of(base + group * SUB, SUB), SUB)


def pack_faces_x(ref, owned, group, x, first, second):
    direction = 1 if x else 0
    ref[at_rows(direction * owned, group), :] = first
    ref[at_rows((2 + direction) * owned, group), :] = second


def pack_faces_y(ref, owned, grid, state_ref, group):
    rows = at_rows(0, group)
    for half in range(2):
        low, high = None, None
        for place in range(SUB):
            first, second = pieces(state_ref, rows, half * SUB + place)
            here = grid.strip == place
            first, second = turn(first, EDGE * place), turn(second, EDGE * (place + 1))
            low = first if place == 0 else jnp.where(here, first, low)
            high = second if place == 0 else jnp.where(here, second, high)
        ref[at_rows(2 * half * owned, group), :] = low
        ref[at_rows((2 * half + 1) * owned, group), :] = high


def placed(send_ref, faces, coded):
    if coded:
        rows = picked(send_ref[...], encode(faces))
    else:
        rows = jnp.dot(
            send_ref[...], faces.astype(jnp.bfloat16), preferred_element_type=jnp.float32
        )
    return rows.reshape(rows.shape[0] // ROWS, ROWS, LANES)


def taken(matrix, message, coded):
    rows = message.shape[0] * ROWS
    if coded:
        level = message.astype(jnp.int32).astype(jnp.float32).reshape(rows, LANES)
        return decode(picked(matrix, level))
    return jnp.dot(
        matrix,
        message.astype(jnp.float32).reshape(rows, LANES).astype(jnp.bfloat16),
        preferred_element_type=jnp.float32,
    )


def as_codes(parts):
    return jnp.concatenate(parts, axis=1).astype(jnp.int32).astype(jnp.int16)


def groups(owned, body):
    def step(group, carry):
        body(group)
        return carry

    lax.fori_loop(0, owned // SUB, step, 0)


def pack_kernel(incoming, members, dest_ref, now_hbm, old_hbm, out_ref, held, arrived):
    slots = dest_ref.shape[1]
    cells = now_hbm.shape[1]
    width = cells // CHUNKS
    copies = []
    for chunk in range(CHUNKS):
        for index, ref in ((0, now_hbm), (1, old_hbm)):
            number = 2 * chunk + index
            copy = pltpu.make_async_copy(
                ref.at[:, pl.ds(chunk * width, width)], held.at[number], arrived.at[number]
            )
            copy.start()
            copies.append(copy)
    dest = dest_ref[...]
    src = lax.broadcasted_iota(jnp.int32, (slots, slots), 1)
    other = lax.broadcasted_iota(jnp.int32, (slots, slots), 0)
    across = jnp.broadcast_to(dest, (slots, slots))
    down = jnp.sum(jnp.where(src == other, across, 0), axis=1, keepdims=True)
    receiver = jnp.zeros((1, slots), jnp.int32)
    for member in range(1, members):
        receiver = receiver + (dest >= member * incoming).astype(jnp.int32)
    earlier = (down >= receiver * incoming) & (down < dest)
    place = jnp.sum(earlier.astype(jnp.int32), axis=0, keepdims=True)
    spot = jnp.where(dest >= 0, receiver * CAP + place, -1)
    chosen = jnp.where(other == spot, 1.0, 0.0).astype(jnp.bfloat16)
    for number, copy in enumerate(copies):
        copy.wait()
        rows = jnp.dot(chosen, held[number], preferred_element_type=jnp.float32)
        out_ref[:, :, number * width : (number + 1) * width] = rows.astype(jnp.bfloat16).reshape(
            members, CAP, width
        )


def prepare_kernel(height_ref, column_ref, count_ref, mask_ref):
    owned = height_ref.shape[0]
    row = lax.broadcasted_iota(jnp.int32, (FACE, FACE), 0)
    column = lax.broadcasted_iota(jnp.int32, (FACE, FACE), 1)
    level = (lax.broadcasted_iota(jnp.int32, (owned, FACE), 1) % EDGE).astype(jnp.float32)
    heights = height_ref[...].astype(jnp.bfloat16)
    for x in range(EDGE):
        spread = jnp.where(row == column // EDGE + x * EDGE, 1.0, 0.0).astype(jnp.bfloat16)
        floor = jnp.dot(heights, spread, preferred_element_type=jnp.float32)
        mask_ref[:, x * FACE : (x + 1) * FACE] = jnp.where(level >= floor, 1.0, 0.0)

    def count(group):
        rows = at_rows(0, group)
        columns = column_ref[rows, :]
        near = [
            jnp.broadcast_to(columns[:, at : at + 1], (SUB, LANES))
            for at in range(NEAR, NEAR + 6)
        ]
        grid = Grid(near[4] + near[5])
        for x in range(EDGE):
            total = grid.total(
                lambda at: pieces(mask_ref, rows, at),
                x,
                lambda at: (near[1], near[1]) if at else (near[0], near[0]),
                lambda at: (near[2], near[3]),
            )
            air = pieces(mask_ref, rows, x)
            for half in range(2):
                at = slice(x * FACE + half * LANES, x * FACE + (half + 1) * LANES)
                count_ref[rows, at] = jnp.where(air[half] > 0.0, total[half], -1.0)

    groups(owned, count)


def one_hot(numbers, shape, axis):
    at = lax.broadcasted_iota(jnp.int32, shape, axis).astype(jnp.float32)
    return jnp.where(numbers == at, 1.0, 0.0).astype(jnp.bfloat16)


def begin_kernel(
    got_hbm,
    own_hbm,
    count_hbm,
    column_ref,
    send_at_ref,
    p_ref,
    p_ends_ref,
    q_ref,
    q_ends_ref,
    out_ref,
    send_x_ref,
    send_y_ref,
    got,
    own,
    count,
    x_ref,
    y_ref,
    arrived,
):
    members = got_hbm.shape[0]
    owned, cells = p_ref.shape
    kept = own_hbm.shape[0] // 2
    width = cells // CHUNKS
    copies = [
        pltpu.make_async_copy(own_hbm, own, arrived.at[2 * CHUNKS]),
        pltpu.make_async_copy(count_hbm, count, arrived.at[2 * CHUNKS + 1]),
    ]
    for number in range(2 * CHUNKS):
        copies.append(
            pltpu.make_async_copy(
                got_hbm.at[:, :, pl.ds(number * width, width)], got.at[number], arrived.at[number]
            )
        )
    for copy in copies:
        copy.start()
    columns = column_ref[...]
    chosen = one_hot(columns[:, INBOX : INBOX + 1], (owned, members * CAP), 1)
    order = columns[:, ORDER : ORDER + 1]
    stay = [
        one_hot(jnp.where(order < kept, order + index * kept, -1.0), (owned, 2 * kept), 1)
        for index in range(2)
    ]
    number = 2 * 2 * owned
    for index, ref in enumerate((send_x_ref, send_y_ref)):
        ref[...] = one_hot(send_at_ref[index : index + 1, :], (members * ROWS, number), 0)
    copies[0].wait()
    copies[1].wait()
    for chunk in range(CHUNKS):
        at = slice(chunk * width, (chunk + 1) * width)
        air = jnp.where(count[:, at] >= 0.0, 1.0, 0.0)
        for index, to_ref in enumerate((p_ref, q_ref)):
            copies[2 + 2 * chunk + index].wait()
            rows = jnp.dot(
                chosen,
                got[2 * chunk + index].reshape(members * CAP, width),
                preferred_element_type=jnp.float32,
            )
            rows = rows + jnp.dot(stay[index], own[:, at], preferred_element_type=jnp.float32)
            to_ref[:, at] = air * rows
    for ref, ends_ref in ((p_ref, p_ends_ref), (q_ref, q_ends_ref)):
        ends_ref[:, :FACE] = ref[:, :FACE]
        ends_ref[:, FACE:] = ref[:, cells - FACE :]
    grid = Grid(jnp.ones((SUB, LANES), jnp.float32))

    def faces(group):
        for x in (0, EDGE - 1):
            pack_faces_x(x_ref, owned, group, x, *pieces(p_ref, at_rows(0, group), x))
        pack_faces_y(y_ref, owned, grid, p_ref, group)

    groups(owned, faces)
    parts = [placed(send_x_ref, x_ref[...], False), placed(send_y_ref, y_ref[...], False)]
    out_ref[...] = jnp.concatenate(parts, axis=1).astype(jnp.bfloat16)


def inner_kernel(
    coded,
    last,
    here_ref,
    take_ref,
    column_ref,
    p_ref,
    p_ends_ref,
    q_ref,
    q_ends_ref,
    keep_ref,
    gain_ref,
    lag_ref,
    new_ref,
    y_ref,
    ghost_ref,
):
    owned = p_ref.shape[0]
    ghost_ref[...] = taken(take_ref[...], here_ref[:, ROWS:, :], coded)

    def advance(group):
        rows = at_rows(0, group)
        grid = Grid(jnp.broadcast_to(column_ref[rows, JOINED : JOINED + 1], (SUB, LANES)))
        low, high = (
            [ghost_ref[at_rows((2 * half + d) * owned, group), :] for half in range(2)]
            for d in range(2)
        )

        def ghost_y(x):
            half, place = x // SUB, x % SUB
            return turn(low[half], -EDGE * place), turn(high[half], -EDGE * (place + 1))

        for x in range(EDGE):
            total = grid.total(lambda at: plane(p_ref, p_ends_ref, rows, at), x, None, ghost_y)
            state = plane(p_ref, p_ends_ref, rows, x)
            lagging = plane(q_ref, q_ends_ref, rows, x)
            keep = pieces(keep_ref, rows, x)
            gain = pieces(gain_ref, rows, x)
            lag = pieces(lag_ref, rows, x)
            for h in range(2):
                new_ref[rows, x * FACE + h * LANES : x * FACE + (h + 1) * LANES] = (
                    keep[h] * state[h] + gain[h] * total[h] - lag[h] * lagging[h]
                )

    groups(owned, advance)
    if not last:
        grid = Grid(jnp.ones((SUB, LANES), jnp.float32))
        groups(owned, lambda group: pack_faces_y(y_ref, owned, grid, new_ref, group))


def first_inner_kernel(
    here_ref,
    take_at_ref,
    column_ref,
    count_hbm,
    p_ref,
    p_ends_ref,
    q_ref,
    q_ends_ref,
    part_ref,
    y_ref,
    take_y_ref,
    take_low_ref,
    take_high_ref,
    keep_ref,
    gain_ref,
    lag_ref,
    count,
    ghost_ref,
    arrived,
):
    owned = p_ref.shape[0]
    copy = pltpu.make_async_copy(count_hbm, count, arrived.at[0])
    copy.start()
    message_rows = here_ref.shape[0] * ROWS
    first = 0
    for ref in (take_y_ref, take_low_ref, take_high_ref):
        number = ref.shape[0]
        ref[...] = one_hot(take_at_ref[first : first + number, :], (number, message_rows), 1)
        first += number
    copy.wait()

    def fields(group):
        rows = at_rows(0, group)
        rate = jnp.broadcast_to(column_ref[rows, RATE : RATE + 1], (SUB, LANES))
        for x in range(EDGE):
            for half, opened in enumerate(pieces(count, rows, x)):
                air = jnp.where(opened >= 0.0, 1.0, 0.0)
                damping = courant * (6.0 - opened) * rate / 2.0
                share = air / (1.0 + damping)
                at = slice(x * FACE + half * LANES, x * FACE + (half + 1) * LANES)
                keep_ref[rows, at] = (2.0 - opened * courant_sq) * share
                gain_ref[rows, at] = courant_sq * share
                lag_ref[rows, at] = (1.0 - damping) * share

    groups(owned, fields)
    inner_kernel(
        False, False, here_ref, take_y_ref, column_ref, p_ref, p_ends_ref, q_ref, q_ends_ref,
        keep_ref, gain_ref, lag_ref, part_ref, y_ref, ghost_ref,
    )


def last_inner_kernel(*refs):
    inner_kernel(True, True, *refs[:-1], None, refs[-1])


def outer_kernel(
    coded,
    last,
    low_ref,
    high_ref,
    take_low_ref,
    take_high_ref,
    gain_ref,
    part_ref,
    y_ref,
    send_x_ref,
    send_y_ref,
    ends_ref,
    out_ref,
    ghost_low,
    ghost_high,
    x_ref,
    y_out,
):
    owned = part_ref.shape[0]
    ghost_low[...] = taken(take_low_ref[...], low_ref[...], coded)
    ghost_high[...] = taken(take_high_ref[...], high_ref[...], coded)
    grid = Grid(jnp.ones((SUB, LANES), jnp.float32))
    if not last:
        y_out[...] = y_ref[...]

    def finish(group):
        rows = at_rows(0, group)
        for x, ghost in ((0, ghost_low), (EDGE - 1, ghost_high)):
            part = pieces(part_ref, rows, x)
            gain = pieces(gain_ref, rows, x)
            done = [
                part[h] + gain[h] * ghost[at_rows(h * owned, group), :] for h in range(2)
            ]
            for h in range(2):
                at = (FACE if x else 0) + h * LANES
                ends_ref[rows, at : at + LANES] = done[h]
            if last:
                continue
            pack_faces_x(x_ref, owned, group, x, *done)
            half, place = x // SUB, x % SUB
            here = grid.strip == place
            for d, face in enumerate(
                (turn(done[0], EDGE * place), turn(done[1], EDGE * (place + 1)))
            ):
                at = at_rows((2 * half + d) * owned, group)
                y_out[at, :] = jnp.where(here, face, y_out[at, :])

    groups(owned, finish)
    if not last:
        out_ref[...] = as_codes(
            [placed(send_x_ref, x_ref[...], True), placed(send_y_ref, y_out[...], True)]
        )


def last_outer_kernel(
    low_ref, high_ref, take_low_ref, take_high_ref, gain_ref, part_ref, place_ref, out_ref, a, b, ends
):
    outer_kernel(
        True, True, low_ref, high_ref, take_low_ref, take_high_ref, gain_ref, part_ref,
        None, None, None, ends, None, a, b, None, None,
    )
    owned, cells = part_ref.shape
    back = one_hot(place_ref[...], (owned, owned), 1)
    out_ref[:, FACE : cells - FACE] = picked(back, part_ref[:, FACE : cells - FACE])
    out_ref[:, :FACE] = picked(back, ends[:, :FACE])
    out_ref[:, cells - FACE :] = picked(back, ends[:, FACE:])


def on_device(
    resident_now,
    resident_old,
    source_now,
    source_old,
    destination,
    anchor,
    floor_height,
    admit_class,
    admittance,
    neighbours,
):
    members = lax.axis_size("dom")
    slabs = lax.axis_size("slab")
    owned = floor_height.shape[0]
    incoming = anchor.shape[0]
    cells = source_now.shape[1]
    kept = owned - incoming
    f32, bf16, i32 = jnp.float32, jnp.bfloat16, jnp.int32

    width = cells // CHUNKS
    outgoing = pl.pallas_call(
        functools.partial(pack_kernel, incoming, members),
        out_shape=jax.ShapeDtypeStruct((members, CAP, 2 * cells), bf16),
        in_specs=[
            pl.BlockSpec(memory_space=pltpu.VMEM),
            pl.BlockSpec(memory_space=pltpu.HBM),
            pl.BlockSpec(memory_space=pltpu.HBM),
        ],
        scratch_shapes=[
            pltpu.VMEM((2 * CHUNKS, source_now.shape[0], width), bf16),
            pltpu.SemaphoreType.DMA((2 * CHUNKS,)),
        ],
        compiler_params=pltpu.CompilerParams(vmem_limit_bytes=60 * 1024 * 1024),
    )(destination[None, :], source_now, source_old)
    got = lax.all_to_all(outgoing, "dom", split_axis=0, concat_axis=0, tiled=True)

    present = neighbours >= 0
    peer_dev = neighbours // owned % members
    peer_slot = neighbours % owned
    slot_ids = jnp.arange(owned, dtype=i32)
    lower = present[5]
    upper = present[4]
    lower_rank = jnp.sum((lower[None, :] & (slot_ids[None, :] < slot_ids[:, None])).astype(i32), axis=1)
    partner_rank = jnp.sum(
        (lower[None, :] & (slot_ids[None, :] < peer_slot[4][:, None])).astype(i32), axis=1
    )
    alone = ~(lower | upper)
    alone_rank = jnp.sum((alone[None, :] & (slot_ids[None, :] < slot_ids[:, None])).astype(i32), axis=1)
    pairs = jnp.sum(lower.astype(i32))
    position = jnp.where(
        lower, 2 * lower_rank, jnp.where(upper, 2 * partner_rank + 1, 2 * pairs + alone_rank)
    )
    order_is = position[None, :] == slot_ids[:, None]
    order = jnp.sum(jnp.where(order_is, slot_ids[None, :], 0), axis=1)
    seat = rank_within(anchor, jnp.arange(incoming, dtype=i32), anchor >= 0)
    inbox = jnp.concatenate([jnp.full((kept,), -1, i32), anchor * CAP + seat])
    class_ids = jnp.arange(admittance.shape[0], dtype=i32)
    send_at = []
    take_at = []
    for d in range(DIRS):
        order_out = rank_within(peer_dev[d], peer_slot[d], present[d])
        order_in = rank_within(peer_dev[d], slot_ids, present[d])
        send_at.append(jnp.where(present[d], peer_dev[d] * ROWS + d % 2 * CAP + order_out, -ROWS))
        take_at.append(jnp.where(present[d], peer_dev[d] * ROWS + (d + 1) % 2 * CAP + order_in, -ROWS))
    rates = jnp.sum(
        jnp.where(admit_class[:, None] == class_ids[None, :], admittance[None, :], 0.0), axis=1
    )
    near = [present[d].astype(f32) for d in range(6)]
    table = jnp.stack(
        [number.astype(f32) for number in send_at + take_at + [inbox, slot_ids]]
        + [rates, near[4] + near[5]]
        + near
    )
    table = jnp.sum(jnp.where(order_is[None], table[:, None, :], 0.0), axis=2)
    columns = table[2 * DIRS :].T
    halved = jnp.arange(2, dtype=i32).astype(f32) * (2 * CAP)
    send_at = (table[:DIRS].reshape(2, 1, 2, owned) + halved[None, :, None, None]).reshape(2, -1)
    take_at = jnp.concatenate(
        [
            (table[DIRS + 2 : DIRS + 4][None] + halved[:, None, None]).reshape(-1, 1),
            (table[DIRS : DIRS + 1] + halved[:, None]).reshape(-1, 1),
            (table[DIRS + 1 : DIRS + 2] + halved[:, None]).reshape(-1, 1),
        ]
    )
    place = position[:, None].astype(f32)
    heights = floor_height[order].astype(f32)
    own = jnp.concatenate([resident_now, resident_old])

    hbm = pl.BlockSpec(memory_space=pltpu.HBM)
    near_by = pl.BlockSpec(memory_space=pltpu.VMEM)
    grid_shape = jax.ShapeDtypeStruct((owned, cells), f32)
    count = pl.pallas_call(
        prepare_kernel,
        out_shape=grid_shape,
        scratch_shapes=[pltpu.VMEM((owned, cells), f32)],
        compiler_params=VMEM,
    )(heights, columns)
    got, own, count, columns, send_at, take_at, place = lax.optimization_barrier(
        (got, own, count, columns, send_at, take_at, place)
    )

    message = (members, 2 * ROWS, LANES)
    faces_shape = (2 * 2 * owned, LANES)
    faces_scratch = pltpu.VMEM(faces_shape, f32)
    ghost_scratch = pltpu.VMEM((2 * owned, LANES), f32)
    ends_shape = jax.ShapeDtypeStruct((owned, 2 * FACE), f32)
    message_rows = members * ROWS
    *fields, outbox, send_x, send_y = pl.pallas_call(
        begin_kernel,
        out_shape=[grid_shape, ends_shape] * 2
        + [jax.ShapeDtypeStruct(message, bf16)]
        + [jax.ShapeDtypeStruct((message_rows, faces_shape[0]), bf16)] * 2,
        in_specs=[hbm] * 3 + [near_by] * 2,
        scratch_shapes=[
            pltpu.VMEM((2 * CHUNKS, members, CAP, width), bf16),
            pltpu.VMEM(own.shape, bf16),
            pltpu.VMEM((owned, cells), f32),
            faces_scratch,
            faces_scratch,
            pltpu.SemaphoreType.DMA((2 * CHUNKS + 2,)),
        ],
        compiler_params=VMEM,
    )(got, own, count, columns, send_at)
    state, lagging = fields[:2], fields[2:]
    ends = slabs - 1
    cost = pl.CostEstimate(flops=60 * owned * cells, bytes_accessed=48 * owned * cells, transcendentals=0)
    for sweep in range(ITERS):
        coded = sweep > 0
        here = lax.all_to_all(outbox, "dom", split_axis=0, concat_axis=0, tiled=True)
        across_x = lax.slice_in_dim(here, 0, ROWS, axis=1)
        from_low = lax.ppermute(across_x, "slab", [(i, i + 1) for i in range(ends)])
        from_high = lax.ppermute(across_x, "slab", [(i + 1, i) for i in range(ends)])
        if sweep == 0:
            part, faces, take_y, take_low, take_high, keep, gain, lag = pl.pallas_call(
                first_inner_kernel,
                out_shape=[grid_shape, jax.ShapeDtypeStruct(faces_shape, f32)]
                + [
                    jax.ShapeDtypeStruct((number, message_rows), bf16)
                    for number in (4 * owned, 2 * owned, 2 * owned)
                ]
                + [grid_shape] * 3,
                in_specs=[near_by] * 3 + [hbm] + [near_by] * 4,
                scratch_shapes=[
                    pltpu.VMEM((owned, cells), f32),
                    faces_scratch,
                    pltpu.SemaphoreType.DMA((1,)),
                ],
                compiler_params=VMEM,
                cost_estimate=cost,
            )(here, take_at, columns, count, *state, *lagging)
        fields = (here, take_y, columns, *state, *lagging, keep, gain, lag)
        if 0 < sweep < ITERS - 1:
            part, faces = pl.pallas_call(
                functools.partial(inner_kernel, coded, False),
                out_shape=[grid_shape, jax.ShapeDtypeStruct(faces_shape, f32)],
                scratch_shapes=[faces_scratch],
                compiler_params=VMEM,
                cost_estimate=cost,
            )(*fields)
        if sweep < ITERS - 1:
            edges, outbox = pl.pallas_call(
                functools.partial(outer_kernel, coded, False),
                out_shape=[ends_shape, jax.ShapeDtypeStruct(message, jnp.int16)],
                scratch_shapes=[ghost_scratch, ghost_scratch, faces_scratch, faces_scratch],
                compiler_params=VMEM,
            )(from_low, from_high, take_low, take_high, gain, part, faces, send_x, send_y)
        else:
            part = pl.pallas_call(
                last_inner_kernel,
                out_shape=grid_shape,
                scratch_shapes=[faces_scratch],
                compiler_params=VMEM,
                cost_estimate=cost,
            )(*fields)
            return pl.pallas_call(
                last_outer_kernel,
                out_shape=grid_shape,
                scratch_shapes=[ghost_scratch, ghost_scratch, pltpu.VMEM((owned, 2 * FACE), f32)],
                compiler_params=VMEM,
            )(from_low, from_high, take_low, take_high, gain, part, place)
        lagging, state = state, (part, edges)


def solution(mesh):
    split = P(("slab", "dom"), None)
    line = P(("slab", "dom"))
    return jax.shard_map(
        on_device,
        mesh=mesh,
        in_specs=(split, split, split, split, line, line, split, line, P(), P(None, ("slab", "dom"))),
        out_specs=split,
        check_vma=False,
    )
```

```python
import functools

import jax
import jax.numpy as jnp
from jax import lax
from jax.experimental import pallas as pl
from jax.experimental.pallas import tpu as pltpu
from jax.sharding import PartitionSpec as P

EDGE = 16
CAP = 2
ITERS = 4
FACE = EDGE * EDGE
CELLS = EDGE * FACE
LANES = 128
SUB = 8
DIRS = 4
ROWS = DIRS * CAP
CHUNKS = 4

TAKE, INBOX, ORDER, RATE, JOINED, NEAR = 0, 4, 5, 6, 7, 8

courant_sq = 0.3
courant = 0.3**0.5

OCTAVE = 1024.0
LOWEST = 23.5

VMEM = pltpu.CompilerParams(vmem_limit_bytes=16 * 1024 * 1024)


def rank_within(groups, orderings, usable):
    earlier = (
        (groups[:, None] == groups[None, :])
        & (orderings[None, :] < orderings[:, None])
        & usable[None, :]
    )
    return jnp.sum(earlier.astype(jnp.int32), axis=1)


def encode(values):
    size = jnp.abs(values)
    level = jnp.floor((jnp.log2(jnp.maximum(size, 1e-30)) + LOWEST) * OCTAVE + 0.5)
    level = jnp.clip(level, 0.0, 32767.0)
    return jnp.where(values < 0.0, -level, level)


def decode(level):
    size = jnp.exp2(jnp.abs(level) * (1.0 / OCTAVE) - LOWEST)
    return jnp.where(level > 0.0, size, jnp.where(level < 0.0, -size, 0.0))


def picked(matrix, values):
    high = values.astype(jnp.bfloat16)
    low = (values - high.astype(jnp.float32)).astype(jnp.bfloat16)
    width = values.shape[1]
    if width == LANES:
        both = jnp.dot(
            matrix, jnp.concatenate([high, low], axis=1), preferred_element_type=jnp.float32
        )
        return both[:, :width] + both[:, width:]
    return jnp.dot(matrix, high, preferred_element_type=jnp.float32) + jnp.dot(
        matrix, low, preferred_element_type=jnp.float32
    )


def turn(block, shift, axis=1):
    size = block.shape[axis]
    shift = shift % size
    return pltpu.roll(block, shift, axis) if shift else block


class Grid:
    def __init__(self, joined):
        lane = lax.broadcasted_iota(jnp.int32, (SUB, LANES), 1)
        row = lax.broadcasted_iota(jnp.int32, (SUB, LANES), 0)
        self.first_y = lane < EDGE
        self.last_y = lane >= LANES - EDGE
        self.bottom = lane % EDGE == 0
        self.top = lane % EDGE == EDGE - 1
        self.odd = row % 2 == 1
        self.strip = lane // EDGE
        upper = jnp.where(self.odd, 1.0, 0.0)
        self.joined_down = joined * upper
        self.joined_up = joined * (1.0 - upper)

    def along_z(self, block):
        partner = jnp.where(self.odd, turn(block, 1, 0), turn(block, -1, 0))
        below = jnp.where(
            self.bottom, turn(partner, 1 - EDGE) * self.joined_down, turn(block, 1)
        )
        above = jnp.where(self.top, turn(partner, EDGE - 1) * self.joined_up, turn(block, -1))
        return below + above

    def total(self, plane, x, ghost_x, ghost_y):
        first, second = plane(x)
        sides = [plane(at) for at in (x - 1, x + 1) if 0 <= at < EDGE]
        if ghost_x is not None and x in (0, EDGE - 1):
            sides.append(ghost_x(x))
        along_x = [sum(side[half] for side in sides) for half in range(2)]
        up_first, up_second = turn(first, EDGE), turn(second, EDGE)
        down_first, down_second = turn(first, -EDGE), turn(second, -EDGE)
        low, high = ghost_y(x)
        total_first = (
            along_x[0]
            + (jnp.where(self.first_y, low, up_first) + jnp.where(self.last_y, down_second, down_first))
            + self.along_z(first)
        )
        total_second = (
            along_x[1]
            + (jnp.where(self.first_y, up_first, up_second) + jnp.where(self.last_y, high, down_second))
            + self.along_z(second)
        )
        return total_first, total_second


def pieces(ref, rows, x):
    at = x * FACE
    return ref[rows, at : at + LANES], ref[rows, at + LANES : at + FACE]


def plane(ref, ends_ref, rows, x):
    if x in (0, EDGE - 1):
        return pieces(ends_ref, rows, 1 if x else 0)
    return pieces(ref, rows, x)


def at_rows(base, group):
    return pl.ds(pl.multiple_of(base + group * SUB, SUB), SUB)


def pack_faces_x(ref, owned, group, x, first, second):
    direction = 1 if x else 0
    ref[at_rows(direction * owned, group), :] = first
    ref[at_rows((2 + direction) * owned, group), :] = second


def pack_faces_y(ref, owned, grid, state_ref, group):
    rows = at_rows(0, group)
    for half in range(2):
        low, high = None, None
        for place in range(SUB):
            first, second = pieces(state_ref, rows, half * SUB + place)
            here = grid.strip == place
            first, second = turn(first, EDGE * place), turn(second, EDGE * (place + 1))
            low = first if place == 0 else jnp.where(here, first, low)
            high = second if place == 0 else jnp.where(here, second, high)
        ref[at_rows(2 * half * owned, group), :] = low
        ref[at_rows((2 * half + 1) * owned, group), :] = high


def one_hot(numbers, shape, axis):
    at = lax.broadcasted_iota(jnp.int32, shape, axis).astype(jnp.float32)
    return jnp.where(numbers == at, 1.0, 0.0).astype(jnp.bfloat16)


def placed(matrix, faces, coded):
    if coded:
        rows = picked(matrix, encode(faces))
    else:
        rows = jnp.dot(
            matrix, faces.astype(jnp.bfloat16), preferred_element_type=jnp.float32
        )
    return rows.reshape(rows.shape[0] // ROWS, ROWS, LANES)


def taken(matrix, message, coded):
    rows = message.shape[0] * ROWS
    if coded:
        level = message.astype(jnp.int32).astype(jnp.float32).reshape(rows, LANES)
        return decode(picked(matrix, level))
    return jnp.dot(
        matrix,
        message.astype(jnp.float32).reshape(rows, LANES).astype(jnp.bfloat16),
        preferred_element_type=jnp.float32,
    )


def as_codes(parts):
    return jnp.concatenate(parts, axis=1).astype(jnp.int32).astype(jnp.int16)


def groups(owned, body):
    def step(group, carry):
        body(group)
        return carry

    lax.fori_loop(0, owned // SUB, step, 0)


def pack_kernel(incoming, members, dest_ref, now_hbm, old_hbm, out_ref, held, arrived):
    slots = dest_ref.shape[1]
    cells = now_hbm.shape[1]
    width = cells // CHUNKS
    copies = []
    for chunk in range(CHUNKS):
        for index, ref in ((0, now_hbm), (1, old_hbm)):
            number = 2 * chunk + index
            copy = pltpu.make_async_copy(
                ref.at[:, pl.ds(chunk * width, width)], held.at[number], arrived.at[number]
            )
            copy.start()
            copies.append(copy)
    dest = dest_ref[...]
    src = lax.broadcasted_iota(jnp.int32, (slots, slots), 1)
    other = lax.broadcasted_iota(jnp.int32, (slots, slots), 0)
    across = jnp.broadcast_to(dest, (slots, slots))
    down = jnp.sum(jnp.where(src == other, across, 0), axis=1, keepdims=True)
    receiver = jnp.zeros((1, slots), jnp.int32)
    for member in range(1, members):
        receiver = receiver + (dest >= member * incoming).astype(jnp.int32)
    earlier = (down >= receiver * incoming) & (down < dest)
    place = jnp.sum(earlier.astype(jnp.int32), axis=0, keepdims=True)
    spot = jnp.where(dest >= 0, receiver * CAP + place, -1)
    chosen = jnp.where(other == spot, 1.0, 0.0).astype(jnp.bfloat16)
    for number, copy in enumerate(copies):
        copy.wait()
        rows = jnp.dot(chosen, held[number], preferred_element_type=jnp.float32)
        out_ref[:, :, number * width : (number + 1) * width] = rows.astype(jnp.bfloat16).reshape(
            members, CAP, width
        )


def prepare_kernel(height_ref, column_ref, count_ref, mask_ref):
    owned = height_ref.shape[0]
    row = lax.broadcasted_iota(jnp.int32, (FACE, FACE), 0)
    column = lax.broadcasted_iota(jnp.int32, (FACE, FACE), 1)
    level = (lax.broadcasted_iota(jnp.int32, (owned, FACE), 1) % EDGE).astype(jnp.float32)
    heights = height_ref[...].astype(jnp.bfloat16)
    for x in range(EDGE):
        spread = jnp.where(row == column // EDGE + x * EDGE, 1.0, 0.0).astype(jnp.bfloat16)
        floor = jnp.dot(heights, spread, preferred_element_type=jnp.float32)
        mask_ref[:, x * FACE : (x + 1) * FACE] = jnp.where(level >= floor, 1.0, 0.0)

    def count(group):
        rows = at_rows(0, group)
        columns = column_ref[rows, :]
        near = [
            jnp.broadcast_to(columns[:, at : at + 1], (SUB, LANES))
            for at in range(NEAR, NEAR + 6)
        ]
        grid = Grid(near[4] + near[5])
        for x in range(EDGE):
            total = grid.total(
                lambda at: pieces(mask_ref, rows, at),
                x,
                lambda at: (near[1], near[1]) if at else (near[0], near[0]),
                lambda at: (near[2], near[3]),
            )
            air = pieces(mask_ref, rows, x)
            for half in range(2):
                at = slice(x * FACE + half * LANES, x * FACE + (half + 1) * LANES)
                count_ref[rows, at] = jnp.where(air[half] > 0.0, total[half], -1.0)

    groups(owned, count)


def settled(got_ref, own_ref, columns, index, to_ref, ends_ref, count_ref):
    owned, cells = to_ref.shape
    members = got_ref.shape[0]
    width = cells // CHUNKS
    chosen = one_hot(columns[:, INBOX : INBOX + 1], (owned, members * CAP), 1)
    stay = one_hot(columns[:, ORDER : ORDER + 1], (owned, own_ref.shape[0]), 1)
    for chunk in range(CHUNKS):
        at = slice(chunk * width, (chunk + 1) * width)
        first = (2 * chunk + index) * width
        rows = jnp.dot(
            chosen,
            got_ref[:, :, first : first + width].reshape(members * CAP, width),
            preferred_element_type=jnp.float32,
        )
        rows = rows + jnp.dot(stay, own_ref[:, at], preferred_element_type=jnp.float32)
        to_ref[:, at] = jnp.where(count_ref[:, at] >= 0.0, rows, 0.0)
    ends_ref[:, :FACE] = to_ref[:, :FACE]
    ends_ref[:, FACE:] = to_ref[:, cells - FACE :]


def begin_kernel(
    got_ref, own_ref, count_ref, column_ref, send_at_ref, p_ref, ends_ref, out_ref, x_ref, y_ref
):
    members = got_ref.shape[0]
    owned = p_ref.shape[0]
    settled(got_ref, own_ref, column_ref[...], 0, p_ref, ends_ref, count_ref)
    grid = Grid(jnp.ones((SUB, LANES), jnp.float32))

    def faces(group):
        for x in (0, EDGE - 1):
            pack_faces_x(x_ref, owned, group, x, *pieces(p_ref, at_rows(0, group), x))
        pack_faces_y(y_ref, owned, grid, p_ref, group)

    groups(owned, faces)
    shape = (members * ROWS, 4 * owned)
    parts = [
        placed(one_hot(send_at_ref[index : index + 1, :], shape, 0), ref[...], False)
        for index, ref in enumerate((x_ref, y_ref))
    ]
    out_ref[...] = jnp.concatenate(parts, axis=1).astype(jnp.bfloat16)


def inner_kernel(
    coded,
    last,
    here_ref,
    take_ref,
    column_ref,
    p_ref,
    p_ends_ref,
    q_ref,
    q_ends_ref,
    keep_ref,
    gain_ref,
    lag_ref,
    new_ref,
    y_ref,
    ghost_ref,
):
    owned = p_ref.shape[0]
    ghost_ref[...] = taken(take_ref[...], here_ref[:, ROWS:, :], coded)

    def advance(group):
        rows = at_rows(0, group)
        grid = Grid(jnp.broadcast_to(column_ref[rows, JOINED : JOINED + 1], (SUB, LANES)))
        low, high = (
            [ghost_ref[at_rows((2 * half + d) * owned, group), :] for half in range(2)]
            for d in range(2)
        )

        def ghost_y(x):
            half, place = x // SUB, x % SUB
            return turn(low[half], -EDGE * place), turn(high[half], -EDGE * (place + 1))

        for x in range(EDGE):
            total = grid.total(lambda at: plane(p_ref, p_ends_ref, rows, at), x, None, ghost_y)
            state = plane(p_ref, p_ends_ref, rows, x)
            lagging = plane(q_ref, q_ends_ref, rows, x)
            keep = pieces(keep_ref, rows, x)
            gain = pieces(gain_ref, rows, x)
            lag = pieces(lag_ref, rows, x)
            for h in range(2):
                new_ref[rows, x * FACE + h * LANES : x * FACE + (h + 1) * LANES] = (
                    keep[h] * state[h] + gain[h] * total[h] - lag[h] * lagging[h]
                )

    groups(owned, advance)
    if not last:
        grid = Grid(jnp.ones((SUB, LANES), jnp.float32))
        groups(owned, lambda group: pack_faces_y(y_ref, owned, grid, new_ref, group))


def first_inner_kernel(
    here_ref,
    column_ref,
    send_at_ref,
    got_ref,
    own_ref,
    count_ref,
    p_ref,
    p_ends_ref,
    part_ref,
    y_ref,
    q_ref,
    q_ends_ref,
    take_y_ref,
    take_low_ref,
    take_high_ref,
    send_x_ref,
    send_y_ref,
    keep_ref,
    gain_ref,
    lag_ref,
    ghost_ref,
):
    owned = p_ref.shape[0]
    columns = column_ref[...]
    settled(got_ref, own_ref, columns, 1, q_ref, q_ends_ref, count_ref)
    for ref, directions in ((take_y_ref, (2, 3)), (take_low_ref, (0,)), (take_high_ref, (1,))):
        numbers = [
            columns[:, TAKE + d : TAKE + d + 1] + 2 * CAP * half
            for half in range(2)
            for d in directions
        ]
        ref[...] = one_hot(jnp.concatenate(numbers, axis=0), ref.shape, 1)
    for index, ref in enumerate((send_x_ref, send_y_ref)):
        ref[...] = one_hot(send_at_ref[index : index + 1, :], ref.shape, 0)

    def fields(group):
        rows = at_rows(0, group)
        rate = jnp.broadcast_to(column_ref[rows, RATE : RATE + 1], (SUB, LANES))
        for x in range(EDGE):
            for half, opened in enumerate(pieces(count_ref, rows, x)):
                air = jnp.where(opened >= 0.0, 1.0, 0.0)
                damping = courant * (6.0 - opened) * rate / 2.0
                share = air / (1.0 + damping)
                at = slice(x * FACE + half * LANES, x * FACE + (half + 1) * LANES)
                keep_ref[rows, at] = (2.0 - opened * courant_sq) * share
                gain_ref[rows, at] = courant_sq * share
                lag_ref[rows, at] = (1.0 - damping) * share

    groups(owned, fields)
    inner_kernel(
        False, False, here_ref, take_y_ref, column_ref, p_ref, p_ends_ref, q_ref, q_ends_ref,
        keep_ref, gain_ref, lag_ref, part_ref, y_ref, ghost_ref,
    )


def last_inner_kernel(*refs):
    inner_kernel(True, True, *refs[:-1], None, refs[-1])


def outer_kernel(
    coded,
    last,
    low_ref,
    high_ref,
    take_low_ref,
    take_high_ref,
    gain_ref,
    part_ref,
    y_ref,
    send_x_ref,
    send_y_ref,
    ends_ref,
    out_ref,
    ghost_low,
    ghost_high,
    x_ref,
    y_out,
):
    owned = part_ref.shape[0]
    ghost_low[...] = taken(take_low_ref[...], low_ref[...], coded)
    ghost_high[...] = taken(take_high_ref[...], high_ref[...], coded)
    grid = Grid(jnp.ones((SUB, LANES), jnp.float32))
    if not last:
        y_out[...] = y_ref[...]

    def finish(group):
        rows = at_rows(0, group)
        for x, ghost in ((0, ghost_low), (EDGE - 1, ghost_high)):
            part = pieces(part_ref, rows, x)
            gain = pieces(gain_ref, rows, x)
            done = [
                part[h] + gain[h] * ghost[at_rows(h * owned, group), :] for h in range(2)
            ]
            for h in range(2):
                at = (FACE if x else 0) + h * LANES
                ends_ref[rows, at : at + LANES] = done[h]
            if last:
                continue
            pack_faces_x(x_ref, owned, group, x, *done)
            half, place = x // SUB, x % SUB
            here = grid.strip == place
            for d, face in enumerate(
                (turn(done[0], EDGE * place), turn(done[1], EDGE * (place + 1)))
            ):
                at = at_rows((2 * half + d) * owned, group)
                y_out[at, :] = jnp.where(here, face, y_out[at, :])

    groups(owned, finish)
    if not last:
        out_ref[...] = as_codes(
            [placed(send_x_ref[...], x_ref[...], True), placed(send_y_ref[...], y_out[...], True)]
        )


def last_outer_kernel(
    low_ref, high_ref, take_low_ref, take_high_ref, gain_ref, part_ref, place_ref, out_ref, a, b, ends
):
    outer_kernel(
        True, True, low_ref, high_ref, take_low_ref, take_high_ref, gain_ref, part_ref,
        None, None, None, ends, None, a, b, None, None,
    )
    owned, cells = part_ref.shape
    back = one_hot(place_ref[...], (owned, owned), 1)
    out_ref[:, FACE : cells - FACE] = picked(back, part_ref[:, FACE : cells - FACE])
    out_ref[:, :FACE] = picked(back, ends[:, :FACE])
    out_ref[:, cells - FACE :] = picked(back, ends[:, FACE:])


def on_device(
    resident_now,
    resident_old,
    source_now,
    source_old,
    destination,
    anchor,
    floor_height,
    admit_class,
    admittance,
    neighbours,
):
    members = lax.axis_size("dom")
    slabs = lax.axis_size("slab")
    owned = floor_height.shape[0]
    incoming = anchor.shape[0]
    cells = source_now.shape[1]
    kept = owned - incoming
    f32, bf16, i32 = jnp.float32, jnp.bfloat16, jnp.int32

    width = cells // CHUNKS
    outgoing = pl.pallas_call(
        functools.partial(pack_kernel, incoming, members),
        out_shape=jax.ShapeDtypeStruct((members, CAP, 2 * cells), bf16),
        in_specs=[
            pl.BlockSpec(memory_space=pltpu.VMEM),
            pl.BlockSpec(memory_space=pltpu.HBM),
            pl.BlockSpec(memory_space=pltpu.HBM),
        ],
        scratch_shapes=[
            pltpu.VMEM((2 * CHUNKS, source_now.shape[0], width), bf16),
            pltpu.SemaphoreType.DMA((2 * CHUNKS,)),
        ],
        compiler_params=pltpu.CompilerParams(vmem_limit_bytes=60 * 1024 * 1024),
    )(destination[None, :], source_now, source_old)
    got = lax.all_to_all(outgoing, "dom", split_axis=0, concat_axis=0, tiled=True)

    present = neighbours >= 0
    peer_dev = neighbours // owned % members
    peer_slot = neighbours % owned
    slot_ids = jnp.arange(owned, dtype=i32)
    lower = present[5]
    upper = present[4]
    lower_rank = jnp.sum((lower[None, :] & (slot_ids[None, :] < slot_ids[:, None])).astype(i32), axis=1)
    partner_rank = jnp.sum(
        (lower[None, :] & (slot_ids[None, :] < peer_slot[4][:, None])).astype(i32), axis=1
    )
    alone = ~(lower | upper)
    alone_rank = jnp.sum((alone[None, :] & (slot_ids[None, :] < slot_ids[:, None])).astype(i32), axis=1)
    pairs = jnp.sum(lower.astype(i32))
    position = jnp.where(
        lower, 2 * lower_rank, jnp.where(upper, 2 * partner_rank + 1, 2 * pairs + alone_rank)
    )
    order_is = position[None, :] == slot_ids[:, None]
    order = jnp.sum(jnp.where(order_is, slot_ids[None, :], 0), axis=1)
    seat = rank_within(anchor, jnp.arange(incoming, dtype=i32), anchor >= 0)
    inbox = jnp.concatenate([jnp.full((kept,), -1, i32), anchor * CAP + seat])
    class_ids = jnp.arange(admittance.shape[0], dtype=i32)
    send_at = []
    take_at = []
    for d in range(DIRS):
        order_out = rank_within(peer_dev[d], peer_slot[d], present[d])
        order_in = rank_within(peer_dev[d], slot_ids, present[d])
        send_at.append(jnp.where(present[d], peer_dev[d] * ROWS + d % 2 * CAP + order_out, -ROWS))
        take_at.append(jnp.where(present[d], peer_dev[d] * ROWS + (d + 1) % 2 * CAP + order_in, -ROWS))
    rates = jnp.sum(
        jnp.where(admit_class[:, None] == class_ids[None, :], admittance[None, :], 0.0), axis=1
    )
    near = [present[d].astype(f32) for d in range(6)]
    table = jnp.stack(
        [number.astype(f32) for number in send_at + take_at + [inbox, slot_ids]]
        + [rates, near[4] + near[5]]
        + near
    )
    table = jnp.sum(jnp.where(order_is[None], table[:, None, :], 0.0), axis=2)
    columns = table[DIRS:].T
    halved = jnp.arange(2, dtype=i32).astype(f32) * (2 * CAP)
    send_at = (table[:DIRS].reshape(2, 1, 2, owned) + halved[None, :, None, None]).reshape(2, -1)
    place = position[:, None].astype(f32)
    heights = floor_height[order].astype(f32)

    grid_shape = jax.ShapeDtypeStruct((owned, cells), f32)
    count = pl.pallas_call(
        prepare_kernel,
        out_shape=grid_shape,
        scratch_shapes=[pltpu.VMEM((owned, cells), f32)],
        compiler_params=VMEM,
    )(heights, columns)
    got, count, columns, send_at, place = lax.optimization_barrier(
        (got, count, columns, send_at, place)
    )

    message = (members, 2 * ROWS, LANES)
    faces_shape = (2 * 2 * owned, LANES)
    faces_scratch = pltpu.VMEM(faces_shape, f32)
    ghost_scratch = pltpu.VMEM((2 * owned, LANES), f32)
    ends_shape = jax.ShapeDtypeStruct((owned, 2 * FACE), f32)
    message_rows = members * ROWS
    *state, outbox = pl.pallas_call(
        begin_kernel,
        out_shape=[grid_shape, ends_shape, jax.ShapeDtypeStruct(message, bf16)],
        scratch_shapes=[faces_scratch, faces_scratch],
        compiler_params=VMEM,
    )(got, resident_now, count, columns, send_at)

    cost = pl.CostEstimate(flops=60 * owned * cells, bytes_accessed=48 * owned * cells, transcendentals=0)
    for sweep in range(ITERS):
        coded = sweep > 0
        here = lax.all_to_all(outbox, "dom", split_axis=0, concat_axis=0, tiled=True)
        across_x = lax.slice_in_dim(here, 0, ROWS, axis=1)
        from_low = lax.ppermute(across_x, "slab", [(i, (i + 1) % slabs) for i in range(slabs)])
        from_high = lax.ppermute(across_x, "slab", [((i + 1) % slabs, i) for i in range(slabs)])
        if sweep == 0:
            part, faces, *lagging, take_y, take_low, take_high, send_x, send_y, keep, gain, lag = (
                pl.pallas_call(
                    first_inner_kernel,
                    out_shape=[grid_shape, jax.ShapeDtypeStruct(faces_shape, f32)]
                    + [grid_shape, ends_shape]
                    + [
                        jax.ShapeDtypeStruct((number, message_rows), bf16)
                        for number in (4 * owned, 2 * owned, 2 * owned)
                    ]
                    + [jax.ShapeDtypeStruct((message_rows, 4 * owned), bf16)] * 2
                    + [grid_shape] * 3,
                    scratch_shapes=[faces_scratch],
                    compiler_params=VMEM,
                    cost_estimate=cost,
                )(here, columns, send_at, got, resident_old, count, *state)
            )
        if sweep:
            fields = (here, take_y, columns, *state, *lagging, keep, gain, lag)
        if 0 < sweep < ITERS - 1:
            part, faces = pl.pallas_call(
                functools.partial(inner_kernel, coded, False),
                out_shape=[grid_shape, jax.ShapeDtypeStruct(faces_shape, f32)],
                scratch_shapes=[faces_scratch],
                compiler_params=VMEM,
                cost_estimate=cost,
            )(*fields)
        if sweep < ITERS - 1:
            edges, outbox = pl.pallas_call(
                functools.partial(outer_kernel, coded, False),
                out_shape=[ends_shape, jax.ShapeDtypeStruct(message, jnp.int16)],
                scratch_shapes=[ghost_scratch, ghost_scratch, faces_scratch, faces_scratch],
                compiler_params=VMEM,
            )(from_low, from_high, take_low, take_high, gain, part, faces, send_x, send_y)
        else:
            part = pl.pallas_call(
                last_inner_kernel,
                out_shape=grid_shape,
                scratch_shapes=[faces_scratch],
                compiler_params=VMEM,
                cost_estimate=cost,
            )(*fields)
            return pl.pallas_call(
                last_outer_kernel,
                out_shape=grid_shape,
                scratch_shapes=[ghost_scratch, ghost_scratch, pltpu.VMEM((owned, 2 * FACE), f32)],
                compiler_params=VMEM,
            )(from_low, from_high, take_low, take_high, gain, part, place)
        lagging, state = state, (part, edges)


def solution(mesh):
    split = P(("slab", "dom"), None)
    line = P(("slab", "dom"))
    return jax.shard_map(
        on_device,
        mesh=mesh,
        in_specs=(split, split, split, split, line, line, split, line, P(), P(None, ("slab", "dom"))),
        out_specs=split,
        check_vma=False,
    )
```

```python
import functools

import jax
import jax.numpy as jnp
from jax import lax
from jax.experimental import pallas as pl
from jax.experimental.pallas import tpu as pltpu
from jax.sharding import PartitionSpec as P

EDGE = 16
CAP = 2
ITERS = 4
FACE = EDGE * EDGE
CELLS = EDGE * FACE
LANES = 128
SUB = 8
DIRS = 4
ROWS = DIRS * CAP
CHUNKS = 4

STEP = (2 * CAP, CAP)
HALF = (CAP, 2 * CAP)
PITCH = (ROWS // 2, ROWS)

TAKE, INBOX, ORDER, RATE, JOINED, NEAR = 0, 4, 5, 6, 7, 8

courant_sq = 0.3
courant = 0.3**0.5

OCTAVE = 1024.0
LOWEST = 23.5

VMEM = pltpu.CompilerParams(vmem_limit_bytes=16 * 1024 * 1024)


def rank_within(groups, orderings, usable):
    earlier = (
        (groups[:, None] == groups[None, :])
        & (orderings[None, :] < orderings[:, None])
        & usable[None, :]
    )
    return jnp.sum(earlier.astype(jnp.int32), axis=1)


def encode(values):
    size = jnp.abs(values)
    level = jnp.floor((jnp.log2(jnp.maximum(size, 1e-30)) + LOWEST) * OCTAVE + 0.5)
    level = jnp.clip(level, 0.0, 32767.0)
    return jnp.where(values < 0.0, -level, level)


def decode(level):
    size = jnp.exp2(jnp.abs(level) * (1.0 / OCTAVE) - LOWEST)
    return jnp.where(level > 0.0, size, jnp.where(level < 0.0, -size, 0.0))


def picked(matrix, values):
    high = values.astype(jnp.bfloat16)
    low = (values - high.astype(jnp.float32)).astype(jnp.bfloat16)
    width = values.shape[1]
    if width == LANES:
        both = jnp.dot(
            matrix, jnp.concatenate([high, low], axis=1), preferred_element_type=jnp.float32
        )
        return both[:, :width] + both[:, width:]
    return jnp.dot(matrix, high, preferred_element_type=jnp.float32) + jnp.dot(
        matrix, low, preferred_element_type=jnp.float32
    )


def turn(block, shift, axis=1):
    size = block.shape[axis]
    shift = shift % size
    return pltpu.roll(block, shift, axis) if shift else block


class Grid:
    def __init__(self, joined):
        lane = lax.broadcasted_iota(jnp.int32, (SUB, LANES), 1)
        row = lax.broadcasted_iota(jnp.int32, (SUB, LANES), 0)
        self.first_y = lane < EDGE
        self.last_y = lane >= LANES - EDGE
        self.bottom = lane % EDGE == 0
        self.top = lane % EDGE == EDGE - 1
        self.odd = row % 2 == 1
        self.strip = lane // EDGE
        upper = jnp.where(self.odd, 1.0, 0.0)
        self.joined_down = joined * upper
        self.joined_up = joined * (1.0 - upper)

    def along_z(self, block):
        partner = jnp.where(self.odd, turn(block, 1, 0), turn(block, -1, 0))
        below = jnp.where(
            self.bottom, turn(partner, 1 - EDGE) * self.joined_down, turn(block, 1)
        )
        above = jnp.where(self.top, turn(partner, EDGE - 1) * self.joined_up, turn(block, -1))
        return below + above

    def total(self, plane, x, ghost_x, ghost_y):
        first, second = plane(x)
        sides = [plane(at) for at in (x - 1, x + 1) if 0 <= at < EDGE]
        if ghost_x is not None and x in (0, EDGE - 1):
            sides.append(ghost_x(x))
        along_x = [sum(side[half] for side in sides) for half in range(2)]
        up_first, up_second = turn(first, EDGE), turn(second, EDGE)
        down_first, down_second = turn(first, -EDGE), turn(second, -EDGE)
        low, high = ghost_y(x)
        total_first = (
            along_x[0]
            + (jnp.where(self.first_y, low, up_first) + jnp.where(self.last_y, down_second, down_first))
            + self.along_z(first)
        )
        total_second = (
            along_x[1]
            + (jnp.where(self.first_y, up_first, up_second) + jnp.where(self.last_y, high, down_second))
            + self.along_z(second)
        )
        return total_first, total_second


def pieces(ref, rows, x):
    at = x * FACE
    return ref[rows, at : at + LANES], ref[rows, at + LANES : at + FACE]


def plane(ref, ends_ref, rows, x):
    if x in (0, EDGE - 1):
        return pieces(ends_ref, rows, 1 if x else 0)
    return pieces(ref, rows, x)


def at_rows(base, group):
    return pl.ds(pl.multiple_of(base + group * SUB, SUB), SUB)


def pack_faces_x(ref, owned, group, x, first, second):
    direction = 1 if x else 0
    ref[at_rows(direction * owned, group), :] = first
    ref[at_rows((2 + direction) * owned, group), :] = second


def pack_faces_y(ref, owned, grid, state_ref, group):
    rows = at_rows(0, group)
    for half in range(2):
        low, high = None, None
        for place in range(SUB):
            first, second = pieces(state_ref, rows, half * SUB + place)
            here = grid.strip == place
            first, second = turn(first, EDGE * place), turn(second, EDGE * (place + 1))
            low = first if place == 0 else jnp.where(here, first, low)
            high = second if place == 0 else jnp.where(here, second, high)
        ref[at_rows(2 * half * owned, group), :] = low
        ref[at_rows((2 * half + 1) * owned, group), :] = high


def one_hot(numbers, shape, axis):
    at = lax.broadcasted_iota(jnp.int32, shape, axis).astype(jnp.float32)
    return jnp.where(numbers == at, 1.0, 0.0).astype(jnp.bfloat16)


def placed(matrix, faces, coded):
    if coded:
        rows = picked(matrix, encode(faces))
    else:
        rows = jnp.dot(
            matrix, faces.astype(jnp.bfloat16), preferred_element_type=jnp.float32
        )
    return rows.reshape(rows.shape[0] // ROWS, ROWS, LANES)


def taken(matrix, message, coded, first=0):
    if coded:
        message = message.astype(jnp.int32)
    message = message.astype(jnp.float32)[:, first:, :]
    message = message.reshape(message.shape[0] * message.shape[1], LANES)
    if coded:
        return decode(picked(matrix, message))
    return jnp.dot(matrix, message.astype(jnp.bfloat16), preferred_element_type=jnp.float32)


def as_codes(parts):
    return jnp.concatenate(parts, axis=1).astype(jnp.int32).astype(jnp.int16)


def groups(owned, body):
    def step(group, carry):
        body(group)
        return carry

    lax.fori_loop(0, owned // SUB, step, 0)


def pack_kernel(
    incoming, members, dest_hbm, now_hbm, old_hbm, out_ref, dest_ref, held, arrived
):
    slots = dest_ref.shape[1]
    cells = now_hbm.shape[1]
    width = cells // CHUNKS
    copies = []
    first = pltpu.make_async_copy(dest_hbm, dest_ref, arrived.at[2 * CHUNKS])
    first.start()
    for chunk in range(CHUNKS):
        for index, ref in ((0, now_hbm), (1, old_hbm)):
            number = 2 * chunk + index
            copy = pltpu.make_async_copy(
                ref.at[:, pl.ds(chunk * width, width)], held.at[number], arrived.at[number]
            )
            copy.start()
            copies.append(copy)
    first.wait()
    dest = dest_ref[...]
    src = lax.broadcasted_iota(jnp.int32, (slots, slots), 1)
    other = lax.broadcasted_iota(jnp.int32, (slots, slots), 0)
    across = jnp.broadcast_to(dest, (slots, slots))
    down = jnp.sum(jnp.where(src == other, across, 0), axis=1, keepdims=True)
    receiver = jnp.zeros((1, slots), jnp.int32)
    for member in range(1, members):
        receiver = receiver + (dest >= member * incoming).astype(jnp.int32)
    earlier = (down >= receiver * incoming) & (down < dest)
    place = jnp.sum(earlier.astype(jnp.int32), axis=0, keepdims=True)
    spot = jnp.where(dest >= 0, receiver * CAP + place, -1)
    chosen = jnp.where(other == spot, 1.0, 0.0).astype(jnp.bfloat16)
    for number, copy in enumerate(copies):
        copy.wait()
        rows = jnp.dot(chosen, held[number], preferred_element_type=jnp.float32)
        out_ref[:, :, number * width : (number + 1) * width] = rows.astype(jnp.bfloat16).reshape(
            members, CAP, width
        )


def prepare_kernel(height_ref, column_ref, count_ref, mask_ref):
    owned = height_ref.shape[0]
    row = lax.broadcasted_iota(jnp.int32, (FACE, FACE), 0)
    column = lax.broadcasted_iota(jnp.int32, (FACE, FACE), 1)
    level = (lax.broadcasted_iota(jnp.int32, (owned, FACE), 1) % EDGE).astype(jnp.float32)
    heights = height_ref[...].astype(jnp.bfloat16)
    for x in range(EDGE):
        spread = jnp.where(row == column // EDGE + x * EDGE, 1.0, 0.0).astype(jnp.bfloat16)
        floor = jnp.dot(heights, spread, preferred_element_type=jnp.float32)
        mask_ref[:, x * FACE : (x + 1) * FACE] = jnp.where(level >= floor, 1.0, 0.0)

    def count(group):
        rows = at_rows(0, group)
        columns = column_ref[rows, :]
        near = [
            jnp.broadcast_to(columns[:, at : at + 1], (SUB, LANES))
            for at in range(NEAR, NEAR + 6)
        ]
        grid = Grid(near[4] + near[5])
        for x in range(EDGE):
            total = grid.total(
                lambda at: pieces(mask_ref, rows, at),
                x,
                lambda at: (near[1], near[1]) if at else (near[0], near[0]),
                lambda at: (near[2], near[3]),
            )
            air = pieces(mask_ref, rows, x)
            for half in range(2):
                at = slice(x * FACE + half * LANES, x * FACE + (half + 1) * LANES)
                count_ref[rows, at] = jnp.where(air[half] > 0.0, total[half], -1.0)

    groups(owned, count)


def settled(got_ref, own_ref, columns, index, to_ref, ends_ref, count_ref):
    owned, cells = to_ref.shape
    members = got_ref.shape[0]
    width = cells // CHUNKS
    chosen = one_hot(columns[:, INBOX : INBOX + 1], (owned, members * CAP), 1)
    stay = one_hot(columns[:, ORDER : ORDER + 1], (owned, own_ref.shape[0]), 1)
    for chunk in range(CHUNKS):
        at = slice(chunk * width, (chunk + 1) * width)
        first = (2 * chunk + index) * width
        rows = jnp.dot(
            chosen,
            got_ref[:, :, first : first + width].reshape(members * CAP, width),
            preferred_element_type=jnp.float32,
        )
        rows = rows + jnp.dot(stay, own_ref[:, at], preferred_element_type=jnp.float32)
        to_ref[:, at] = jnp.where(count_ref[:, at] >= 0.0, rows, 0.0)
    ends_ref[:, :FACE] = to_ref[:, :FACE]
    ends_ref[:, FACE:] = to_ref[:, cells - FACE :]


def begin_kernel(
    got_ref, own_ref, count_ref, column_ref, send_at_ref, p_ref, ends_ref, out_ref, x_ref, y_ref
):
    members = got_ref.shape[0]
    owned = p_ref.shape[0]
    settled(got_ref, own_ref, column_ref[...], 0, p_ref, ends_ref, count_ref)
    grid = Grid(jnp.ones((SUB, LANES), jnp.float32))

    def faces(group):
        for x in (0, EDGE - 1):
            pack_faces_x(x_ref, owned, group, x, *pieces(p_ref, at_rows(0, group), x))
        pack_faces_y(y_ref, owned, grid, p_ref, group)

    groups(owned, faces)
    shape = (members * ROWS, 4 * owned)
    parts = [
        placed(one_hot(send_at_ref[index : index + 1, :], shape, 0), ref[...], False)
        for index, ref in enumerate((x_ref, y_ref))
    ]
    out_ref[...] = jnp.concatenate(parts, axis=1).astype(jnp.bfloat16)


def inner_kernel(
    coded,
    last,
    here_ref,
    take_ref,
    column_ref,
    p_ref,
    p_ends_ref,
    q_ref,
    q_ends_ref,
    keep_ref,
    gain_ref,
    lag_ref,
    new_ref,
    y_ref,
    ghost_ref,
):
    owned = p_ref.shape[0]
    ghost_ref[...] = taken(take_ref[...], here_ref[...], coded, ROWS)

    def advance(group):
        rows = at_rows(0, group)
        grid = Grid(jnp.broadcast_to(column_ref[rows, JOINED : JOINED + 1], (SUB, LANES)))
        low, high = (
            [ghost_ref[at_rows((2 * half + d) * owned, group), :] for half in range(2)]
            for d in range(2)
        )

        def ghost_y(x):
            half, place = x // SUB, x % SUB
            return turn(low[half], -EDGE * place), turn(high[half], -EDGE * (place + 1))

        for x in range(EDGE):
            total = grid.total(lambda at: plane(p_ref, p_ends_ref, rows, at), x, None, ghost_y)
            state = plane(p_ref, p_ends_ref, rows, x)
            lagging = plane(q_ref, q_ends_ref, rows, x)
            keep = pieces(keep_ref, rows, x)
            gain = pieces(gain_ref, rows, x)
            lag = pieces(lag_ref, rows, x)
            for h in range(2):
                new_ref[rows, x * FACE + h * LANES : x * FACE + (h + 1) * LANES] = (
                    keep[h] * state[h] + gain[h] * total[h] - lag[h] * lagging[h]
                )

    groups(owned, advance)
    if not last:
        grid = Grid(jnp.ones((SUB, LANES), jnp.float32))
        groups(owned, lambda group: pack_faces_y(y_ref, owned, grid, new_ref, group))


def first_inner_kernel(
    here_ref,
    column_ref,
    send_at_ref,
    got_ref,
    own_ref,
    count_ref,
    p_ref,
    p_ends_ref,
    part_ref,
    y_ref,
    q_ref,
    q_ends_ref,
    take_y_ref,
    take_low_ref,
    take_high_ref,
    send_x_ref,
    send_y_ref,
    keep_ref,
    gain_ref,
    lag_ref,
    ghost_ref,
):
    owned = p_ref.shape[0]
    columns = column_ref[...]
    settled(got_ref, own_ref, columns, 1, q_ref, q_ends_ref, count_ref)
    for ref, directions in ((take_y_ref, (2, 3)), (take_low_ref, (0,)), (take_high_ref, (1,))):
        numbers = [
            columns[:, TAKE + d : TAKE + d + 1] + HALF[d // 2] * half
            for half in range(2)
            for d in directions
        ]
        ref[...] = one_hot(jnp.concatenate(numbers, axis=0), ref.shape, 1)
    for index, ref in enumerate((send_x_ref, send_y_ref)):
        ref[...] = one_hot(send_at_ref[index : index + 1, :], ref.shape, 0)

    def fields(group):
        rows = at_rows(0, group)
        rate = jnp.broadcast_to(column_ref[rows, RATE : RATE + 1], (SUB, LANES))
        for x in range(EDGE):
            for half, opened in enumerate(pieces(count_ref, rows, x)):
                air = jnp.where(opened >= 0.0, 1.0, 0.0)
                damping = courant * (6.0 - opened) * rate / 2.0
                share = air / (1.0 + damping)
                at = slice(x * FACE + half * LANES, x * FACE + (half + 1) * LANES)
                keep_ref[rows, at] = (2.0 - opened * courant_sq) * share
                gain_ref[rows, at] = courant_sq * share
                lag_ref[rows, at] = (1.0 - damping) * share

    groups(owned, fields)
    inner_kernel(
        False, False, here_ref, take_y_ref, column_ref, p_ref, p_ends_ref, q_ref, q_ends_ref,
        keep_ref, gain_ref, lag_ref, part_ref, y_ref, ghost_ref,
    )


def last_inner_kernel(*refs):
    inner_kernel(True, True, *refs[:-1], None, refs[-1])


def outer_kernel(
    coded,
    last,
    low_ref,
    high_ref,
    take_low_ref,
    take_high_ref,
    gain_ref,
    part_ref,
    y_ref,
    send_x_ref,
    send_y_ref,
    ends_ref,
    out_ref,
    ghost_low,
    ghost_high,
    x_ref,
    y_out,
):
    owned = part_ref.shape[0]
    ghost_low[...] = taken(take_low_ref[...], low_ref[...], coded)
    ghost_high[...] = taken(take_high_ref[...], high_ref[...], coded)
    grid = Grid(jnp.ones((SUB, LANES), jnp.float32))
    if not last:
        y_out[...] = y_ref[...]

    def finish(group):
        rows = at_rows(0, group)
        for x, ghost in ((0, ghost_low), (EDGE - 1, ghost_high)):
            part = pieces(part_ref, rows, x)
            gain = pieces(gain_ref, rows, x)
            done = [
                part[h] + gain[h] * ghost[at_rows(h * owned, group), :] for h in range(2)
            ]
            for h in range(2):
                at = (FACE if x else 0) + h * LANES
                ends_ref[rows, at : at + LANES] = done[h]
            if last:
                continue
            pack_faces_x(x_ref, owned, group, x, *done)
            half, place = x // SUB, x % SUB
            here = grid.strip == place
            for d, face in enumerate(
                (turn(done[0], EDGE * place), turn(done[1], EDGE * (place + 1)))
            ):
                at = at_rows((2 * half + d) * owned, group)
                y_out[at, :] = jnp.where(here, face, y_out[at, :])

    groups(owned, finish)
    if not last:
        out_ref[...] = as_codes(
            [placed(send_x_ref[...], x_ref[...], True), placed(send_y_ref[...], y_out[...], True)]
        )


def last_outer_kernel(
    low_ref, high_ref, take_low_ref, take_high_ref, gain_ref, part_ref, place_ref, out_ref, a, b, ends
):
    outer_kernel(
        True, True, low_ref, high_ref, take_low_ref, take_high_ref, gain_ref, part_ref,
        None, None, None, ends, None, a, b, None, None,
    )
    owned, cells = part_ref.shape
    back = one_hot(place_ref[...], (owned, owned), 1)
    out_ref[:, FACE : cells - FACE] = picked(back, part_ref[:, FACE : cells - FACE])
    out_ref[:, :FACE] = picked(back, ends[:, :FACE])
    out_ref[:, cells - FACE :] = picked(back, ends[:, FACE:])


def on_device(
    resident_now,
    resident_old,
    source_now,
    source_old,
    destination,
    anchor,
    floor_height,
    admit_class,
    admittance,
    neighbours,
):
    members = lax.axis_size("dom")
    slabs = lax.axis_size("slab")
    owned = floor_height.shape[0]
    incoming = anchor.shape[0]
    cells = source_now.shape[1]
    kept = owned - incoming
    f32, bf16, i32 = jnp.float32, jnp.bfloat16, jnp.int32

    width = cells // CHUNKS
    outgoing = pl.pallas_call(
        functools.partial(pack_kernel, incoming, members),
        out_shape=jax.ShapeDtypeStruct((members, CAP, 2 * cells), bf16),
        in_specs=[pl.BlockSpec(memory_space=pltpu.HBM)] * 3,
        scratch_shapes=[
            pltpu.VMEM((1, source_now.shape[0]), i32),
            pltpu.VMEM((2 * CHUNKS, source_now.shape[0], width), bf16),
            pltpu.SemaphoreType.DMA((2 * CHUNKS + 1,)),
        ],
        compiler_params=pltpu.CompilerParams(vmem_limit_bytes=60 * 1024 * 1024),
    )(destination[None, :], source_now, source_old)
    got = lax.all_to_all(outgoing, "dom", split_axis=0, concat_axis=0, tiled=True)

    present = neighbours >= 0
    peer_dev = neighbours // owned % members
    peer_slot = neighbours % owned
    slot_ids = jnp.arange(owned, dtype=i32)
    lower = present[5]
    upper = present[4]
    lower_rank = jnp.sum((lower[None, :] & (slot_ids[None, :] < slot_ids[:, None])).astype(i32), axis=1)
    partner_rank = jnp.sum(
        (lower[None, :] & (slot_ids[None, :] < peer_slot[4][:, None])).astype(i32), axis=1
    )
    alone = ~(lower | upper)
    alone_rank = jnp.sum((alone[None, :] & (slot_ids[None, :] < slot_ids[:, None])).astype(i32), axis=1)
    pairs = jnp.sum(lower.astype(i32))
    position = jnp.where(
        lower, 2 * lower_rank, jnp.where(upper, 2 * partner_rank + 1, 2 * pairs + alone_rank)
    )
    order_is = position[None, :] == slot_ids[:, None]
    order = jnp.sum(jnp.where(order_is, slot_ids[None, :], 0), axis=1)
    seat = rank_within(anchor, jnp.arange(incoming, dtype=i32), anchor >= 0)
    inbox = jnp.concatenate([jnp.full((kept,), -1, i32), anchor * CAP + seat])
    class_ids = jnp.arange(admittance.shape[0], dtype=i32)
    send_at = []
    take_at = []
    for d in range(DIRS):
        order_out = rank_within(peer_dev[d], peer_slot[d], present[d])
        order_in = rank_within(peer_dev[d], slot_ids, present[d])
        send_at.append(jnp.where(present[d], peer_dev[d] * ROWS + d % 2 * STEP[d // 2] + order_out, -ROWS))
        take_at.append(jnp.where(present[d], peer_dev[d] * PITCH[d // 2] + (d + 1) % 2 * (d // 2) * CAP + order_in, -ROWS))
    rates = jnp.sum(
        jnp.where(admit_class[:, None] == class_ids[None, :], admittance[None, :], 0.0), axis=1
    )
    near = [present[d].astype(f32) for d in range(6)]
    table = jnp.stack(
        [number.astype(f32) for number in send_at + take_at + [inbox, slot_ids]]
        + [rates, near[4] + near[5]]
        + near
    )
    table = jnp.sum(jnp.where(order_is[None], table[:, None, :], 0.0), axis=2)
    columns = table[DIRS:].T
    halved = jnp.arange(2, dtype=i32).astype(f32)[None, :] * jnp.array(HALF, f32)[:, None]
    send_at = (table[:DIRS].reshape(2, 1, 2, owned) + halved[:, :, None, None]).reshape(2, -1)
    place = position[:, None].astype(f32)
    heights = floor_height[order].astype(f32)

    grid_shape = jax.ShapeDtypeStruct((owned, cells), f32)
    count = pl.pallas_call(
        prepare_kernel,
        out_shape=grid_shape,
        scratch_shapes=[pltpu.VMEM((owned, cells), f32)],
        compiler_params=VMEM,
    )(heights, columns)
    got, count, columns, send_at, place = lax.optimization_barrier(
        (got, count, columns, send_at, place)
    )

    message = (members, 2 * ROWS, LANES)
    faces_shape = (2 * 2 * owned, LANES)
    faces_scratch = pltpu.VMEM(faces_shape, f32)
    ghost_scratch = pltpu.VMEM((2 * owned, LANES), f32)
    ends_shape = jax.ShapeDtypeStruct((owned, 2 * FACE), f32)
    message_rows = members * ROWS
    *state, outbox = pl.pallas_call(
        begin_kernel,
        out_shape=[grid_shape, ends_shape, jax.ShapeDtypeStruct(message, bf16)],
        scratch_shapes=[faces_scratch, faces_scratch],
        compiler_params=VMEM,
    )(got, resident_now, count, columns, send_at)

    cost = pl.CostEstimate(flops=60 * owned * cells, bytes_accessed=48 * owned * cells, transcendentals=0)
    for sweep in range(ITERS):
        coded = sweep > 0
        here = lax.all_to_all(outbox, "dom", split_axis=0, concat_axis=0, tiled=True)
        down = lax.slice_in_dim(here, 0, ROWS // 2, axis=1)
        up = lax.slice_in_dim(here, ROWS // 2, ROWS, axis=1)
        from_low = lax.ppermute(up, "slab", [(i, (i + 1) % slabs) for i in range(slabs)])
        from_high = lax.ppermute(down, "slab", [((i + 1) % slabs, i) for i in range(slabs)])
        if sweep == 0:
            part, faces, *lagging, take_y, take_low, take_high, send_x, send_y, keep, gain, lag = (
                pl.pallas_call(
                    first_inner_kernel,
                    out_shape=[grid_shape, jax.ShapeDtypeStruct(faces_shape, f32)]
                    + [grid_shape, ends_shape]
                    + [
                        jax.ShapeDtypeStruct((number * owned, message_rows // share), bf16)
                        for number, share in ((4, 1), (2, 2), (2, 2))
                    ]
                    + [jax.ShapeDtypeStruct((message_rows, 4 * owned), bf16)] * 2
                    + [grid_shape] * 3,
                    scratch_shapes=[faces_scratch],
                    compiler_params=VMEM,
                    cost_estimate=cost,
                )(here, columns, send_at, got, resident_old, count, *state)
            )
        if sweep:
            fields = (here, take_y, columns, *state, *lagging, keep, gain, lag)
        if 0 < sweep < ITERS - 1:
            part, faces = pl.pallas_call(
                functools.partial(inner_kernel, coded, False),
                out_shape=[grid_shape, jax.ShapeDtypeStruct(faces_shape, f32)],
                scratch_shapes=[faces_scratch],
                compiler_params=VMEM,
                cost_estimate=cost,
            )(*fields)
        if sweep < ITERS - 1:
            edges, outbox = pl.pallas_call(
                functools.partial(outer_kernel, coded, False),
                out_shape=[ends_shape, jax.ShapeDtypeStruct(message, jnp.int16)],
                scratch_shapes=[ghost_scratch, ghost_scratch, faces_scratch, faces_scratch],
                compiler_params=VMEM,
            )(from_low, from_high, take_low, take_high, gain, part, faces, send_x, send_y)
        else:
            part = pl.pallas_call(
                last_inner_kernel,
                out_shape=grid_shape,
                scratch_shapes=[faces_scratch],
                compiler_params=VMEM,
                cost_estimate=cost,
            )(*fields)
            return pl.pallas_call(
                last_outer_kernel,
                out_shape=grid_shape,
                scratch_shapes=[ghost_scratch, ghost_scratch, pltpu.VMEM((owned, 2 * FACE), f32)],
                compiler_params=VMEM,
            )(from_low, from_high, take_low, take_high, gain, part, place)
        lagging, state = state, (part, edges)


def solution(mesh):
    split = P(("slab", "dom"), None)
    line = P(("slab", "dom"))
    return jax.shard_map(
        on_device,
        mesh=mesh,
        in_specs=(split, split, split, split, line, line, split, line, P(), P(None, ("slab", "dom"))),
        out_specs=split,
        check_vma=False,
    )
```

```python
import functools
import math

import jax
import jax.numpy as jnp
from jax import lax
from jax.experimental import pallas as pl
from jax.experimental.pallas import tpu as pltpu
from jax.sharding import PartitionSpec as P

EDGE = 16
CAP = 2
ITERS = 4
FACE = EDGE * EDGE
CELLS = EDGE * FACE
LANES = 128
SUB = 8
DIRS = 4
ROWS = DIRS * CAP
CHUNKS = 4

STEP = (2 * CAP, CAP)
HALF = (CAP, 2 * CAP)
PITCH = (ROWS // 2, ROWS)

TAKE, INBOX, ORDER, RATE, WEIGHT, JOINED, NEAR = 0, 4, 5, 6, 7, 8, 9

courant_sq = 0.3
courant = 0.3**0.5

OCTAVE = 1024.0


def lowest(steps):
    return 32767.0 / OCTAVE - 0.01 - math.log2(6.0 * 3.0**steps)

VMEM = pltpu.CompilerParams(vmem_limit_bytes=16 * 1024 * 1024)


def rank_within(groups, orderings, usable):
    earlier = (
        (groups[:, None] == groups[None, :])
        & (orderings[None, :] < orderings[:, None])
        & usable[None, :]
    )
    return jnp.sum(earlier.astype(jnp.int32), axis=1)


def encode(values, low):
    size = jnp.abs(values)
    level = jnp.floor((jnp.log2(jnp.maximum(size, 1e-30)) + low) * OCTAVE + 0.5)
    level = jnp.clip(level, 0.0, 32767.0)
    return jnp.where(values < 0.0, -level, level)


def decode(level, low):
    size = jnp.exp2(jnp.abs(level) * (1.0 / OCTAVE) - low)
    return jnp.where(level > 0.0, size, jnp.where(level < 0.0, -size, 0.0))


def picked(matrix, values):
    high = values.astype(jnp.bfloat16)
    low = (values - high.astype(jnp.float32)).astype(jnp.bfloat16)
    width = values.shape[1]
    if width == LANES:
        both = jnp.dot(
            matrix, jnp.concatenate([high, low], axis=1), preferred_element_type=jnp.float32
        )
        return both[:, :width] + both[:, width:]
    return jnp.dot(matrix, high, preferred_element_type=jnp.float32) + jnp.dot(
        matrix, low, preferred_element_type=jnp.float32
    )


def turn(block, shift, axis=1):
    size = block.shape[axis]
    shift = shift % size
    return pltpu.roll(block, shift, axis) if shift else block


class Grid:
    def __init__(self, joined):
        lane = lax.broadcasted_iota(jnp.int32, (SUB, LANES), 1)
        row = lax.broadcasted_iota(jnp.int32, (SUB, LANES), 0)
        self.first_y = lane < EDGE
        self.last_y = lane >= LANES - EDGE
        self.bottom = lane % EDGE == 0
        self.top = lane % EDGE == EDGE - 1
        self.odd = row % 2 == 1
        self.strip = lane // EDGE
        upper = jnp.where(self.odd, 1.0, 0.0)
        self.partner = joined * jnp.where(
            self.bottom, upper, jnp.where(self.top, 1.0 - upper, 0.0)
        )

    def along_z(self, block):
        given = jnp.where(self.odd, turn(block, EDGE - 1), turn(block, 1 - EDGE))
        across = jnp.where(self.odd, turn(given, 1, 0), turn(given, -1, 0))
        below = jnp.where(self.bottom, 0.0, turn(block, 1))
        above = jnp.where(self.top, 0.0, turn(block, -1))
        return (below + above) + across * self.partner

    def total(self, plane, x, ghost_x, ghost_y):
        first, second = plane(x)
        sides = [plane(at) for at in (x - 1, x + 1) if 0 <= at < EDGE]
        if ghost_x is not None and x in (0, EDGE - 1):
            sides.append(ghost_x(x))
        along_x = [sum(side[half] for side in sides) for half in range(2)]
        up_first, up_second = turn(first, EDGE), turn(second, EDGE)
        down_first, down_second = turn(first, -EDGE), turn(second, -EDGE)
        low, high = ghost_y(x)
        total_first = (
            along_x[0]
            + (jnp.where(self.first_y, low, up_first) + jnp.where(self.last_y, down_second, down_first))
            + self.along_z(first)
        )
        total_second = (
            along_x[1]
            + (jnp.where(self.first_y, up_first, up_second) + jnp.where(self.last_y, high, down_second))
            + self.along_z(second)
        )
        return total_first, total_second


def pieces(ref, rows, x):
    at = x * FACE
    return ref[rows, at : at + LANES], ref[rows, at + LANES : at + FACE]


def plane(ref, ends_ref, rows, x):
    if x in (0, EDGE - 1):
        return pieces(ends_ref, rows, 1 if x else 0)
    return pieces(ref, rows, x)


def at_rows(base, group):
    return pl.ds(pl.multiple_of(base + group * SUB, SUB), SUB)


def pack_faces_x(ref, owned, group, x, first, second):
    direction = 1 if x else 0
    ref[at_rows(direction * owned, group), :] = first
    ref[at_rows((2 + direction) * owned, group), :] = second


def pack_faces_y(ref, owned, grid, state_ref, group):
    rows = at_rows(0, group)
    for half in range(2):
        low, high = None, None
        for place in range(SUB):
            first, second = pieces(state_ref, rows, half * SUB + place)
            here = grid.strip == place
            first, second = turn(first, EDGE * place), turn(second, EDGE * (place + 1))
            low = first if place == 0 else jnp.where(here, first, low)
            high = second if place == 0 else jnp.where(here, second, high)
        ref[at_rows(2 * half * owned, group), :] = low
        ref[at_rows((2 * half + 1) * owned, group), :] = high


def one_hot(numbers, shape, axis):
    at = lax.broadcasted_iota(jnp.int32, shape, axis).astype(jnp.float32)
    return jnp.where(numbers == at, 1.0, 0.0).astype(jnp.bfloat16)


def placed(matrix, faces, coded):
    if coded:
        rows = picked(matrix, encode(faces, lowest(coded)))
    else:
        rows = jnp.dot(
            matrix, faces.astype(jnp.bfloat16), preferred_element_type=jnp.float32
        )
    return rows.reshape(rows.shape[0] // ROWS, ROWS, LANES)


def taken(matrix, message, coded, first=0):
    if coded:
        message = message.astype(jnp.int32)
    message = message.astype(jnp.float32)[:, first:, :]
    message = message.reshape(message.shape[0] * message.shape[1], LANES)
    if coded:
        return decode(picked(matrix, message), lowest(coded))
    return jnp.dot(matrix, message.astype(jnp.bfloat16), preferred_element_type=jnp.float32)


def as_codes(parts):
    return jnp.concatenate(parts, axis=1).astype(jnp.int32).astype(jnp.int16)


def groups(owned, body):
    def step(group, carry):
        body(group)
        return carry

    lax.fori_loop(0, owned // SUB, step, 0)


def pack_kernel(
    incoming, members, dest_hbm, now_hbm, old_hbm, out_ref, dest_ref, held, arrived
):
    slots = dest_ref.shape[1]
    cells = now_hbm.shape[1]
    width = cells // CHUNKS
    copies = []
    first = pltpu.make_async_copy(dest_hbm, dest_ref, arrived.at[2 * CHUNKS])
    first.start()
    for chunk in range(CHUNKS):
        for index, ref in ((0, now_hbm), (1, old_hbm)):
            number = 2 * chunk + index
            copy = pltpu.make_async_copy(
                ref.at[:, pl.ds(chunk * width, width)], held.at[number], arrived.at[number]
            )
            copy.start()
            copies.append(copy)
    first.wait()
    dest = dest_ref[...]
    src = lax.broadcasted_iota(jnp.int32, (slots, slots), 1)
    other = lax.broadcasted_iota(jnp.int32, (slots, slots), 0)
    across = jnp.broadcast_to(dest, (slots, slots))
    down = jnp.sum(jnp.where(src == other, across, 0), axis=1, keepdims=True)
    receiver = jnp.zeros((1, slots), jnp.int32)
    for member in range(1, members):
        receiver = receiver + (dest >= member * incoming).astype(jnp.int32)
    earlier = (down >= receiver * incoming) & (down < dest)
    place = jnp.sum(earlier.astype(jnp.int32), axis=0, keepdims=True)
    spot = jnp.where(dest >= 0, receiver * CAP + place, -1)
    chosen = jnp.where(other == spot, 1.0, 0.0).astype(jnp.bfloat16)
    for number, copy in enumerate(copies):
        copy.wait()
        rows = jnp.dot(chosen, held[number], preferred_element_type=jnp.float32)
        out_ref[:, :, number * width : (number + 1) * width] = rows.astype(jnp.bfloat16).reshape(
            members, CAP, width
        )


def prepare_kernel(height_ref, column_ref, share_ref, mask_ref):
    owned = height_ref.shape[0]
    row = lax.broadcasted_iota(jnp.int32, (FACE, FACE), 0)
    column = lax.broadcasted_iota(jnp.int32, (FACE, FACE), 1)
    level = (lax.broadcasted_iota(jnp.int32, (owned, FACE), 1) % EDGE).astype(jnp.float32)
    heights = height_ref[...].astype(jnp.bfloat16)
    for x in range(EDGE):
        spread = jnp.where(row == column // EDGE + x * EDGE, 1.0, 0.0).astype(jnp.bfloat16)
        floor = jnp.dot(heights, spread, preferred_element_type=jnp.float32)
        mask_ref[:, x * FACE : (x + 1) * FACE] = jnp.where(level >= floor, 1.0, 0.0)

    def count(group):
        rows = at_rows(0, group)
        columns = column_ref[rows, :]
        near = [
            jnp.broadcast_to(columns[:, at : at + 1], (SUB, LANES))
            for at in range(NEAR, NEAR + 6)
        ]
        rate = jnp.broadcast_to(columns[:, RATE : RATE + 1], (SUB, LANES))
        grid = Grid(near[4] + near[5])
        for x in range(EDGE):
            total = grid.total(
                lambda at: pieces(mask_ref, rows, at),
                x,
                lambda at: (near[1], near[1]) if at else (near[0], near[0]),
                lambda at: (near[2], near[3]),
            )
            air = pieces(mask_ref, rows, x)
            for half in range(2):
                at = slice(x * FACE + half * LANES, x * FACE + (half + 1) * LANES)
                damping = courant * (6.0 - total[half]) * rate / 2.0
                share_ref[rows, at] = air[half] / (1.0 + damping)

    groups(owned, count)


def settled(got_ref, own_ref, columns, index, to_ref, ends_ref, share_ref):
    owned, cells = to_ref.shape
    members = got_ref.shape[0]
    width = cells // CHUNKS
    chosen = one_hot(columns[:, INBOX : INBOX + 1], (owned, members * CAP), 1)
    stay = one_hot(columns[:, ORDER : ORDER + 1], (owned, own_ref.shape[0]), 1)
    for chunk in range(CHUNKS):
        at = slice(chunk * width, (chunk + 1) * width)
        first = (2 * chunk + index) * width
        rows = jnp.dot(
            chosen,
            got_ref[:, :, first : first + width].reshape(members * CAP, width),
            preferred_element_type=jnp.float32,
        )
        rows = rows + jnp.dot(stay, own_ref[:, at], preferred_element_type=jnp.float32)
        to_ref[:, at] = jnp.where(share_ref[:, at] > 0.0, rows, 0.0)
    ends_ref[:, :FACE] = to_ref[:, :FACE]
    ends_ref[:, FACE:] = to_ref[:, cells - FACE :]


def begin_kernel(
    got_ref, own_ref, share_ref, column_ref, send_at_ref, p_ref, ends_ref, out_ref, x_ref, y_ref
):
    members = got_ref.shape[0]
    owned = p_ref.shape[0]
    settled(got_ref, own_ref, column_ref[...], 0, p_ref, ends_ref, share_ref)
    grid = Grid(jnp.ones((SUB, LANES), jnp.float32))

    def faces(group):
        for x in (0, EDGE - 1):
            pack_faces_x(x_ref, owned, group, x, *pieces(p_ref, at_rows(0, group), x))
        pack_faces_y(y_ref, owned, grid, p_ref, group)

    groups(owned, faces)
    shape = (members * ROWS, 4 * owned)
    parts = [
        placed(one_hot(send_at_ref[index : index + 1, :], shape, 0), ref[...], 0)
        for index, ref in enumerate((x_ref, y_ref))
    ]
    out_ref[...] = jnp.concatenate(parts, axis=1).astype(jnp.bfloat16)


def inner_kernel(
    coded,
    last,
    here_ref,
    take_ref,
    column_ref,
    p_ref,
    p_ends_ref,
    q_ref,
    q_ends_ref,
    share_ref,
    new_ref,
    y_ref,
    ghost_ref,
):
    owned = p_ref.shape[0]
    ghost_ref[...] = taken(take_ref[...], here_ref[...], coded, ROWS)

    def advance(group):
        rows = at_rows(0, group)
        grid = Grid(jnp.broadcast_to(column_ref[rows, JOINED : JOINED + 1], (SUB, LANES)))
        weight = jnp.broadcast_to(column_ref[rows, WEIGHT : WEIGHT + 1], (SUB, LANES))
        inward = (2.0 - 6.0 * courant_sq) - weight
        low, high = (
            [ghost_ref[at_rows((2 * half + d) * owned, group), :] for half in range(2)]
            for d in range(2)
        )

        def ghost_y(x):
            half, place = x // SUB, x % SUB
            return turn(low[half], -EDGE * place), turn(high[half], -EDGE * (place + 1))

        for x in range(EDGE):
            total = grid.total(lambda at: plane(p_ref, p_ends_ref, rows, at), x, None, ghost_y)
            state = plane(p_ref, p_ends_ref, rows, x)
            lagging = plane(q_ref, q_ends_ref, rows, x)
            share = pieces(share_ref, rows, x)
            for h in range(2):
                new_ref[rows, x * FACE + h * LANES : x * FACE + (h + 1) * LANES] = share[h] * (
                    inward * state[h] + courant_sq * total[h] - 2.0 * lagging[h]
                ) + (lagging[h] + weight * state[h])

    groups(owned, advance)
    if not last:
        grid = Grid(jnp.ones((SUB, LANES), jnp.float32))
        groups(owned, lambda group: pack_faces_y(y_ref, owned, grid, new_ref, group))


def first_inner_kernel(
    here_ref,
    column_ref,
    send_at_ref,
    got_ref,
    own_ref,
    share_ref,
    p_ref,
    p_ends_ref,
    part_ref,
    y_ref,
    q_ref,
    q_ends_ref,
    take_y_ref,
    take_low_ref,
    take_high_ref,
    send_x_ref,
    send_y_ref,
    ghost_ref,
):
    owned = p_ref.shape[0]
    columns = column_ref[...]
    settled(got_ref, own_ref, columns, 1, q_ref, q_ends_ref, share_ref)
    for ref, directions in ((take_y_ref, (2, 3)), (take_low_ref, (0,)), (take_high_ref, (1,))):
        numbers = [
            columns[:, TAKE + d : TAKE + d + 1] + HALF[d // 2] * half
            for half in range(2)
            for d in directions
        ]
        ref[...] = one_hot(jnp.concatenate(numbers, axis=0), ref.shape, 1)
    for index, ref in enumerate((send_x_ref, send_y_ref)):
        ref[...] = one_hot(send_at_ref[index : index + 1, :], ref.shape, 0)

    inner_kernel(
        0, False, here_ref, take_y_ref, column_ref, p_ref, p_ends_ref, q_ref, q_ends_ref,
        share_ref, part_ref, y_ref, ghost_ref,
    )


def last_inner_kernel(*refs):
    inner_kernel(ITERS - 1, True, *refs[:-1], None, refs[-1])


def outer_kernel(
    coded,
    last,
    low_ref,
    high_ref,
    take_low_ref,
    take_high_ref,
    share_ref,
    part_ref,
    y_ref,
    send_x_ref,
    send_y_ref,
    ends_ref,
    out_ref,
    ghost_low,
    ghost_high,
    x_ref,
    y_out,
):
    owned = part_ref.shape[0]
    ghost_low[...] = taken(take_low_ref[...], low_ref[...], coded)
    ghost_high[...] = taken(take_high_ref[...], high_ref[...], coded)
    grid = Grid(jnp.ones((SUB, LANES), jnp.float32))
    if not last:
        y_out[...] = y_ref[...]

    def finish(group):
        rows = at_rows(0, group)
        for x, ghost in ((0, ghost_low), (EDGE - 1, ghost_high)):
            part = pieces(part_ref, rows, x)
            share = pieces(share_ref, rows, x)
            done = [
                part[h] + courant_sq * share[h] * ghost[at_rows(h * owned, group), :] for h in range(2)
            ]
            for h in range(2):
                at = (FACE if x else 0) + h * LANES
                ends_ref[rows, at : at + LANES] = done[h]
            if last:
                continue
            pack_faces_x(x_ref, owned, group, x, *done)
            half, place = x // SUB, x % SUB
            here = grid.strip == place
            for d, face in enumerate(
                (turn(done[0], EDGE * place), turn(done[1], EDGE * (place + 1)))
            ):
                at = at_rows((2 * half + d) * owned, group)
                y_out[at, :] = jnp.where(here, face, y_out[at, :])

    groups(owned, finish)
    if not last:
        out_ref[...] = as_codes(
            [
                placed(send_x_ref[...], x_ref[...], coded + 1),
                placed(send_y_ref[...], y_out[...], coded + 1),
            ]
        )


def last_outer_kernel(
    low_ref, high_ref, take_low_ref, take_high_ref, share_ref, part_ref, place_ref, out_ref, a, b, ends
):
    outer_kernel(
        ITERS - 1, True, low_ref, high_ref, take_low_ref, take_high_ref, share_ref, part_ref,
        None, None, None, ends, None, a, b, None, None,
    )
    owned, cells = part_ref.shape
    back = one_hot(place_ref[...], (owned, owned), 1)
    out_ref[:, FACE : cells - FACE] = picked(back, part_ref[:, FACE : cells - FACE])
    out_ref[:, :FACE] = picked(back, ends[:, :FACE])
    out_ref[:, cells - FACE :] = picked(back, ends[:, FACE:])


def on_device(
    resident_now,
    resident_old,
    source_now,
    source_old,
    destination,
    anchor,
    floor_height,
    admit_class,
    admittance,
    neighbours,
):
    members = lax.axis_size("dom")
    slabs = lax.axis_size("slab")
    owned = floor_height.shape[0]
    incoming = anchor.shape[0]
    cells = source_now.shape[1]
    kept = owned - incoming
    f32, bf16, i32 = jnp.float32, jnp.bfloat16, jnp.int32

    width = cells // CHUNKS
    outgoing = pl.pallas_call(
        functools.partial(pack_kernel, incoming, members),
        out_shape=jax.ShapeDtypeStruct((members, CAP, 2 * cells), bf16),
        in_specs=[pl.BlockSpec(memory_space=pltpu.HBM)] * 3,
        scratch_shapes=[
            pltpu.VMEM((1, source_now.shape[0]), i32),
            pltpu.VMEM((2 * CHUNKS, source_now.shape[0], width), bf16),
            pltpu.SemaphoreType.DMA((2 * CHUNKS + 1,)),
        ],
        compiler_params=pltpu.CompilerParams(vmem_limit_bytes=60 * 1024 * 1024),
    )(destination[None, :], source_now, source_old)
    got = lax.all_to_all(outgoing, "dom", split_axis=0, concat_axis=0, tiled=True)

    present = neighbours >= 0
    peer_dev = neighbours // owned % members
    peer_slot = neighbours % owned
    slot_ids = jnp.arange(owned, dtype=i32)
    lower = present[5]
    upper = present[4]
    lower_rank = jnp.sum((lower[None, :] & (slot_ids[None, :] < slot_ids[:, None])).astype(i32), axis=1)
    partner_rank = jnp.sum(
        (lower[None, :] & (slot_ids[None, :] < peer_slot[4][:, None])).astype(i32), axis=1
    )
    alone = ~(lower | upper)
    alone_rank = jnp.sum((alone[None, :] & (slot_ids[None, :] < slot_ids[:, None])).astype(i32), axis=1)
    pairs = jnp.sum(lower.astype(i32))
    position = jnp.where(
        lower, 2 * lower_rank, jnp.where(upper, 2 * partner_rank + 1, 2 * pairs + alone_rank)
    )
    order_is = position[None, :] == slot_ids[:, None]
    order = jnp.sum(jnp.where(order_is, slot_ids[None, :], 0), axis=1)
    seat = rank_within(anchor, jnp.arange(incoming, dtype=i32), anchor >= 0)
    inbox = jnp.concatenate([jnp.full((kept,), -1, i32), anchor * CAP + seat])
    class_ids = jnp.arange(admittance.shape[0], dtype=i32)
    send_at = []
    take_at = []
    for d in range(DIRS):
        order_out = rank_within(peer_dev[d], peer_slot[d], present[d])
        order_in = rank_within(peer_dev[d], slot_ids, present[d])
        send_at.append(jnp.where(present[d], peer_dev[d] * ROWS + d % 2 * STEP[d // 2] + order_out, -ROWS))
        take_at.append(jnp.where(present[d], peer_dev[d] * PITCH[d // 2] + (d + 1) % 2 * (d // 2) * CAP + order_in, -ROWS))
    rates = jnp.sum(
        jnp.where(admit_class[:, None] == class_ids[None, :], admittance[None, :], 0.0), axis=1
    )
    near = [present[d].astype(f32) for d in range(6)]
    table = jnp.stack(
        [number.astype(f32) for number in send_at + take_at + [inbox, slot_ids]]
        + [rates, 2.0 * courant_sq / (courant * rates), near[4] + near[5]]
        + near
    )
    table = jnp.sum(jnp.where(order_is[None], table[:, None, :], 0.0), axis=2)
    columns = table[DIRS:].T
    halved = jnp.arange(2, dtype=i32).astype(f32)[None, :] * jnp.array(HALF, f32)[:, None]
    send_at = (table[:DIRS].reshape(2, 1, 2, owned) + halved[:, :, None, None]).reshape(2, -1)
    place = position[:, None].astype(f32)
    heights = floor_height[order].astype(f32)

    grid_shape = jax.ShapeDtypeStruct((owned, cells), f32)
    share = pl.pallas_call(
        prepare_kernel,
        out_shape=grid_shape,
        scratch_shapes=[pltpu.VMEM((owned, cells), f32)],
        compiler_params=VMEM,
    )(heights, columns)
    got, share, columns, send_at, place = lax.optimization_barrier(
        (got, share, columns, send_at, place)
    )

    message = (members, 2 * ROWS, LANES)
    faces_shape = (2 * 2 * owned, LANES)
    faces_scratch = pltpu.VMEM(faces_shape, f32)
    ghost_scratch = pltpu.VMEM((2 * owned, LANES), f32)
    ends_shape = jax.ShapeDtypeStruct((owned, 2 * FACE), f32)
    message_rows = members * ROWS
    *state, outbox = pl.pallas_call(
        begin_kernel,
        out_shape=[grid_shape, ends_shape, jax.ShapeDtypeStruct(message, bf16)],
        scratch_shapes=[faces_scratch, faces_scratch],
        compiler_params=VMEM,
    )(got, resident_now, share, columns, send_at)

    cost = pl.CostEstimate(flops=60 * owned * cells, bytes_accessed=48 * owned * cells, transcendentals=0)
    for sweep in range(ITERS):
        here = lax.all_to_all(outbox, "dom", split_axis=0, concat_axis=0, tiled=True)
        down = lax.slice_in_dim(here, 0, ROWS // 2, axis=1)
        up = lax.slice_in_dim(here, ROWS // 2, ROWS, axis=1)
        from_low = lax.ppermute(up, "slab", [(i, (i + 1) % slabs) for i in range(slabs)])
        from_high = lax.ppermute(down, "slab", [((i + 1) % slabs, i) for i in range(slabs)])
        if sweep == 0:
            part, faces, *lagging, take_y, take_low, take_high, send_x, send_y = (
                pl.pallas_call(
                    first_inner_kernel,
                    out_shape=[grid_shape, jax.ShapeDtypeStruct(faces_shape, f32)]
                    + [grid_shape, ends_shape]
                    + [
                        jax.ShapeDtypeStruct((number * owned, message_rows // share), bf16)
                        for number, share in ((4, 1), (2, 2), (2, 2))
                    ]
                    + [jax.ShapeDtypeStruct((message_rows, 4 * owned), bf16)] * 2,
                    scratch_shapes=[faces_scratch],
                    compiler_params=VMEM,
                    cost_estimate=cost,
                )(here, columns, send_at, got, resident_old, share, *state)
            )
        if sweep:
            fields = (here, take_y, columns, *state, *lagging, share)
        if 0 < sweep < ITERS - 1:
            part, faces = pl.pallas_call(
                functools.partial(inner_kernel, sweep, False),
                out_shape=[grid_shape, jax.ShapeDtypeStruct(faces_shape, f32)],
                scratch_shapes=[faces_scratch],
                compiler_params=VMEM,
                cost_estimate=cost,
            )(*fields)
        if sweep < ITERS - 1:
            edges, outbox = pl.pallas_call(
                functools.partial(outer_kernel, sweep, False),
                out_shape=[ends_shape, jax.ShapeDtypeStruct(message, jnp.int16)],
                scratch_shapes=[ghost_scratch, ghost_scratch, faces_scratch, faces_scratch],
                compiler_params=VMEM,
            )(from_low, from_high, take_low, take_high, share, part, faces, send_x, send_y)
        else:
            part = pl.pallas_call(
                last_inner_kernel,
                out_shape=grid_shape,
                scratch_shapes=[faces_scratch],
                compiler_params=VMEM,
                cost_estimate=cost,
            )(*fields)
            return pl.pallas_call(
                last_outer_kernel,
                out_shape=grid_shape,
                scratch_shapes=[ghost_scratch, ghost_scratch, pltpu.VMEM((owned, 2 * FACE), f32)],
                compiler_params=VMEM,
            )(from_low, from_high, take_low, take_high, share, part, place)
        lagging, state = state, (part, edges)


def solution(mesh):
    split = P(("slab", "dom"), None)
    line = P(("slab", "dom"))
    return jax.shard_map(
        on_device,
        mesh=mesh,
        in_specs=(split, split, split, split, line, line, split, line, P(), P(None, ("slab", "dom"))),
        out_specs=split,
        check_vma=False,
    )
```

```python
import functools
import math

import jax
import jax.numpy as jnp
from jax import lax
from jax.experimental import pallas as pl
from jax.experimental.pallas import tpu as pltpu
from jax.sharding import PartitionSpec as P

EDGE = 16
CAP = 2
ITERS = 4
FACE = EDGE * EDGE
CELLS = EDGE * FACE
LANES = 128
SUB = 8
DIRS = 4
ROWS = DIRS * CAP

STEP = (2 * CAP, CAP)
HALF = (CAP, 2 * CAP)
PITCH = (ROWS // 2, ROWS)

TAKE, INBOX, ORDER, RATE, WEIGHT, JOINED, NEAR = 0, 4, 5, 6, 7, 8, 9

courant_sq = 0.3
courant = 0.3**0.5

OCTAVE = 1024.0


def lowest(steps):
    return 32767.0 / OCTAVE - 0.01 - math.log2(6.0 * 3.0**steps)

VMEM = pltpu.CompilerParams(vmem_limit_bytes=16 * 1024 * 1024)


def rank_within(groups, orderings, usable):
    earlier = (
        (groups[:, None] == groups[None, :])
        & (orderings[None, :] < orderings[:, None])
        & usable[None, :]
    )
    return jnp.sum(earlier.astype(jnp.int32), axis=1)


def encode(values, low):
    size = jnp.abs(values)
    level = jnp.floor((jnp.log2(jnp.maximum(size, 1e-30)) + low) * OCTAVE + 0.5)
    level = jnp.clip(level, 0.0, 32767.0)
    return jnp.where(values < 0.0, -level, level)


def decode(level, low):
    size = jnp.exp2(jnp.abs(level) * (1.0 / OCTAVE) - low)
    return jnp.where(level > 0.0, size, jnp.where(level < 0.0, -size, 0.0))


def picked(matrix, values):
    high = values.astype(jnp.bfloat16)
    low = (values - high.astype(jnp.float32)).astype(jnp.bfloat16)
    width = values.shape[1]
    if width == LANES:
        both = jnp.dot(
            matrix, jnp.concatenate([high, low], axis=1), preferred_element_type=jnp.float32
        )
        return both[:, :width] + both[:, width:]
    return jnp.dot(matrix, high, preferred_element_type=jnp.float32) + jnp.dot(
        matrix, low, preferred_element_type=jnp.float32
    )


def turn(block, shift, axis=1):
    size = block.shape[axis]
    shift = shift % size
    return pltpu.roll(block, shift, axis) if shift else block


class Grid:
    def __init__(self, joined):
        lane = lax.broadcasted_iota(jnp.int32, (SUB, LANES), 1)
        row = lax.broadcasted_iota(jnp.int32, (SUB, LANES), 0)
        self.first_y = lane < EDGE
        self.last_y = lane >= LANES - EDGE
        self.bottom = lane % EDGE == 0
        self.top = lane % EDGE == EDGE - 1
        self.odd = row % 2 == 1
        self.strip = lane // EDGE
        upper = jnp.where(self.odd, 1.0, 0.0)
        self.partner = joined * jnp.where(
            self.bottom, upper, jnp.where(self.top, 1.0 - upper, 0.0)
        )

    def along_z(self, block):
        given = jnp.where(self.odd, turn(block, EDGE - 1), turn(block, 1 - EDGE))
        across = jnp.where(self.odd, turn(given, 1, 0), turn(given, -1, 0))
        below = jnp.where(self.bottom, 0.0, turn(block, 1))
        above = jnp.where(self.top, 0.0, turn(block, -1))
        return (below + above) + across * self.partner

    def total(self, plane, x, ghost_x, ghost_y):
        first, second = plane(x)
        sides = [plane(at) for at in (x - 1, x + 1) if 0 <= at < EDGE]
        if ghost_x is not None and x in (0, EDGE - 1):
            sides.append(ghost_x(x))
        along_x = [sum(side[half] for side in sides) for half in range(2)]
        up_first, up_second = turn(first, EDGE), turn(second, EDGE)
        down_first, down_second = turn(first, -EDGE), turn(second, -EDGE)
        low, high = ghost_y(x)
        total_first = (
            along_x[0]
            + (jnp.where(self.first_y, low, up_first) + jnp.where(self.last_y, down_second, down_first))
            + self.along_z(first)
        )
        total_second = (
            along_x[1]
            + (jnp.where(self.first_y, up_first, up_second) + jnp.where(self.last_y, high, down_second))
            + self.along_z(second)
        )
        return total_first, total_second


def pieces(ref, rows, x):
    at = x * FACE
    return ref[rows, at : at + LANES], ref[rows, at + LANES : at + FACE]


def plane(ref, ends_ref, rows, x):
    if x in (0, EDGE - 1):
        return pieces(ends_ref, rows, 1 if x else 0)
    return pieces(ref, rows, x)


def at_rows(base, group):
    return pl.ds(pl.multiple_of(base + group * SUB, SUB), SUB)


def pack_faces_x(ref, owned, group, x, first, second):
    direction = 1 if x else 0
    ref[at_rows(direction * owned, group), :] = first
    ref[at_rows((2 + direction) * owned, group), :] = second


def pack_faces_y(ref, owned, grid, state_ref, group):
    rows = at_rows(0, group)
    for half in range(2):
        low, high = None, None
        for place in range(SUB):
            first, second = pieces(state_ref, rows, half * SUB + place)
            here = grid.strip == place
            first, second = turn(first, EDGE * place), turn(second, EDGE * (place + 1))
            low = first if place == 0 else jnp.where(here, first, low)
            high = second if place == 0 else jnp.where(here, second, high)
        ref[at_rows(2 * half * owned, group), :] = low
        ref[at_rows((2 * half + 1) * owned, group), :] = high


def one_hot(numbers, shape, axis):
    at = lax.broadcasted_iota(jnp.int32, shape, axis).astype(jnp.float32)
    return jnp.where(numbers == at, 1.0, 0.0).astype(jnp.bfloat16)


def placed(matrix, faces, coded):
    if coded:
        rows = picked(matrix, encode(faces, lowest(coded)))
    else:
        rows = jnp.dot(
            matrix, faces.astype(jnp.bfloat16), preferred_element_type=jnp.float32
        )
    return rows.reshape(rows.shape[0] // ROWS, ROWS, LANES)


def taken(matrix, message, coded, first=0):
    if coded:
        message = message.astype(jnp.int32)
    message = message.astype(jnp.float32)[:, first:, :]
    message = message.reshape(message.shape[0] * message.shape[1], LANES)
    if coded:
        return decode(picked(matrix, message), lowest(coded))
    return jnp.dot(matrix, message.astype(jnp.bfloat16), preferred_element_type=jnp.float32)


def as_codes(parts):
    return jnp.concatenate(parts, axis=1).astype(jnp.int32).astype(jnp.int16)


def groups(owned, body):
    def step(group, carry):
        body(group)
        return carry

    lax.fori_loop(0, owned // SUB, step, 0)


def pack_kernel(
    incoming, members, dest_hbm, now_hbm, old_hbm, out_ref, dest_ref, chosen_ref, held, arrived
):
    level = pl.program_id(0)
    slots = dest_ref.shape[1]
    copies = [
        pltpu.make_async_copy(now_hbm, held.at[0], arrived.at[0]),
        pltpu.make_async_copy(old_hbm, held.at[1], arrived.at[1]),
    ]

    @pl.when(level == 0)
    def _():
        first = pltpu.make_async_copy(dest_hbm, dest_ref, arrived.at[2])
        first.start()
        for copy in copies:
            copy.start()
        first.wait()
        dest = dest_ref[...]
        src = lax.broadcasted_iota(jnp.int32, (slots, slots), 1)
        other = lax.broadcasted_iota(jnp.int32, (slots, slots), 0)
        across = jnp.broadcast_to(dest, (slots, slots))
        down = jnp.sum(jnp.where(src == other, across, 0), axis=1, keepdims=True)
        receiver = jnp.zeros((1, slots), jnp.int32)
        for member in range(1, members):
            receiver = receiver + (dest >= member * incoming).astype(jnp.int32)
        earlier = (down >= receiver * incoming) & (down < dest)
        place = jnp.sum(earlier.astype(jnp.int32), axis=0, keepdims=True)
        spot = jnp.where(dest >= 0, receiver * CAP + place, -1)
        chosen_ref[...] = jnp.where(other == spot, 1.0, 0.0).astype(jnp.bfloat16)
        copies[0].wait()

    @pl.when(level == 1)
    def _():
        copies[1].wait()

    rows = jnp.dot(chosen_ref[...], held[level], preferred_element_type=jnp.float32)
    out_ref[...] = rows.astype(jnp.bfloat16).reshape(out_ref.shape)


def prepare_kernel(height_ref, column_ref, share_ref, mask_ref):
    owned = height_ref.shape[0]
    row = lax.broadcasted_iota(jnp.int32, (FACE, FACE), 0)
    column = lax.broadcasted_iota(jnp.int32, (FACE, FACE), 1)
    level = (lax.broadcasted_iota(jnp.int32, (owned, FACE), 1) % EDGE).astype(jnp.float32)
    heights = height_ref[...].astype(jnp.bfloat16)
    for x in range(EDGE):
        spread = jnp.where(row == column // EDGE + x * EDGE, 1.0, 0.0).astype(jnp.bfloat16)
        floor = jnp.dot(heights, spread, preferred_element_type=jnp.float32)
        mask_ref[:, x * FACE : (x + 1) * FACE] = jnp.where(level >= floor, 1.0, 0.0)

    def count(group):
        rows = at_rows(0, group)
        columns = column_ref[rows, :]
        near = [
            jnp.broadcast_to(columns[:, at : at + 1], (SUB, LANES))
            for at in range(NEAR, NEAR + 6)
        ]
        rate = jnp.broadcast_to(columns[:, RATE : RATE + 1], (SUB, LANES))
        grid = Grid(near[4] + near[5])
        for x in range(EDGE):
            total = grid.total(
                lambda at: pieces(mask_ref, rows, at),
                x,
                lambda at: (near[1], near[1]) if at else (near[0], near[0]),
                lambda at: (near[2], near[3]),
            )
            air = pieces(mask_ref, rows, x)
            for half in range(2):
                at = slice(x * FACE + half * LANES, x * FACE + (half + 1) * LANES)
                damping = courant * (6.0 - total[half]) * rate / 2.0
                share_ref[rows, at] = air[half] / (1.0 + damping)

    groups(owned, count)


def settled(got_ref, own_ref, columns, index, to_ref, ends_ref, share_ref):
    owned, cells = to_ref.shape
    members = got_ref.shape[0]
    chosen = one_hot(columns[:, INBOX : INBOX + 1], (owned, members * CAP), 1)
    stay = one_hot(columns[:, ORDER : ORDER + 1], (owned, own_ref.shape[0]), 1)
    arrived = got_ref[:, :, index * cells : (index + 1) * cells].reshape(members * CAP, cells)
    rows = jnp.dot(chosen, arrived, preferred_element_type=jnp.float32)
    rows = rows + jnp.dot(stay, own_ref[...], preferred_element_type=jnp.float32)
    to_ref[...] = jnp.where(share_ref[...] > 0.0, rows, 0.0)
    ends_ref[:, :FACE] = to_ref[:, :FACE]
    ends_ref[:, FACE:] = to_ref[:, cells - FACE :]


def begin_kernel(
    got_ref, own_ref, share_ref, column_ref, send_at_ref, p_ref, ends_ref, out_ref, x_ref, y_ref
):
    members = got_ref.shape[0]
    owned = p_ref.shape[0]
    settled(got_ref, own_ref, column_ref[...], 0, p_ref, ends_ref, share_ref)
    grid = Grid(jnp.ones((SUB, LANES), jnp.float32))

    def faces(group):
        for x in (0, EDGE - 1):
            pack_faces_x(x_ref, owned, group, x, *pieces(p_ref, at_rows(0, group), x))
        pack_faces_y(y_ref, owned, grid, p_ref, group)

    groups(owned, faces)
    shape = (members * ROWS, 4 * owned)
    parts = [
        placed(one_hot(send_at_ref[index : index + 1, :], shape, 0), ref[...], 0)
        for index, ref in enumerate((x_ref, y_ref))
    ]
    out_ref[...] = jnp.concatenate(parts, axis=1).astype(jnp.bfloat16)


def inner_kernel(
    coded,
    last,
    here_ref,
    take_ref,
    column_ref,
    p_ref,
    p_ends_ref,
    q_ref,
    q_ends_ref,
    share_ref,
    new_ref,
    y_ref,
    ghost_ref,
):
    owned = p_ref.shape[0]
    ghost_ref[...] = taken(take_ref[...], here_ref[...], coded, ROWS)

    def advance(group):
        rows = at_rows(0, group)
        grid = Grid(jnp.broadcast_to(column_ref[rows, JOINED : JOINED + 1], (SUB, LANES)))
        weight = jnp.broadcast_to(column_ref[rows, WEIGHT : WEIGHT + 1], (SUB, LANES))
        inward = (2.0 - 6.0 * courant_sq) - weight
        low, high = (
            [ghost_ref[at_rows((2 * half + d) * owned, group), :] for half in range(2)]
            for d in range(2)
        )

        def ghost_y(x):
            half, place = x // SUB, x % SUB
            return turn(low[half], -EDGE * place), turn(high[half], -EDGE * (place + 1))

        for x in range(EDGE):
            total = grid.total(lambda at: plane(p_ref, p_ends_ref, rows, at), x, None, ghost_y)
            state = plane(p_ref, p_ends_ref, rows, x)
            lagging = plane(q_ref, q_ends_ref, rows, x)
            share = pieces(share_ref, rows, x)
            for h in range(2):
                new_ref[rows, x * FACE + h * LANES : x * FACE + (h + 1) * LANES] = share[h] * (
                    inward * state[h] + courant_sq * total[h] - 2.0 * lagging[h]
                ) + (lagging[h] + weight * state[h])

    groups(owned, advance)
    if not last:
        grid = Grid(jnp.ones((SUB, LANES), jnp.float32))
        groups(owned, lambda group: pack_faces_y(y_ref, owned, grid, new_ref, group))


def first_inner_kernel(
    here_ref,
    column_ref,
    send_at_ref,
    got_ref,
    own_ref,
    share_ref,
    p_ref,
    p_ends_ref,
    part_ref,
    y_ref,
    q_ref,
    q_ends_ref,
    take_y_ref,
    take_low_ref,
    take_high_ref,
    send_x_ref,
    send_y_ref,
    ghost_ref,
):
    owned = p_ref.shape[0]
    columns = column_ref[...]
    settled(got_ref, own_ref, columns, 1, q_ref, q_ends_ref, share_ref)
    for ref, directions in ((take_y_ref, (2, 3)), (take_low_ref, (0,)), (take_high_ref, (1,))):
        numbers = [
            columns[:, TAKE + d : TAKE + d + 1] + HALF[d // 2] * half
            for half in range(2)
            for d in directions
        ]
        ref[...] = one_hot(jnp.concatenate(numbers, axis=0), ref.shape, 1)
    for index, ref in enumerate((send_x_ref, send_y_ref)):
        ref[...] = one_hot(send_at_ref[index : index + 1, :], ref.shape, 0)

    inner_kernel(
        0, False, here_ref, take_y_ref, column_ref, p_ref, p_ends_ref, q_ref, q_ends_ref,
        share_ref, part_ref, y_ref, ghost_ref,
    )


def last_inner_kernel(*refs):
    inner_kernel(ITERS - 1, True, *refs[:-1], None, refs[-1])


def outer_kernel(
    coded,
    last,
    low_ref,
    high_ref,
    take_low_ref,
    take_high_ref,
    share_ref,
    part_ref,
    y_ref,
    send_x_ref,
    send_y_ref,
    ends_ref,
    out_ref,
    ghost_low,
    ghost_high,
    x_ref,
    y_out,
):
    owned = part_ref.shape[0]
    ghost_low[...] = taken(take_low_ref[...], low_ref[...], coded)
    ghost_high[...] = taken(take_high_ref[...], high_ref[...], coded)
    grid = Grid(jnp.ones((SUB, LANES), jnp.float32))
    if not last:
        y_out[...] = y_ref[...]

    def finish(group):
        rows = at_rows(0, group)
        for x, ghost in ((0, ghost_low), (EDGE - 1, ghost_high)):
            part = pieces(part_ref, rows, x)
            share = pieces(share_ref, rows, x)
            done = [
                part[h] + courant_sq * share[h] * ghost[at_rows(h * owned, group), :] for h in range(2)
            ]
            for h in range(2):
                at = (FACE if x else 0) + h * LANES
                ends_ref[rows, at : at + LANES] = done[h]
            if last:
                continue
            pack_faces_x(x_ref, owned, group, x, *done)
            half, place = x // SUB, x % SUB
            here = grid.strip == place
            for d, face in enumerate(
                (turn(done[0], EDGE * place), turn(done[1], EDGE * (place + 1)))
            ):
                at = at_rows((2 * half + d) * owned, group)
                y_out[at, :] = jnp.where(here, face, y_out[at, :])

    groups(owned, finish)
    if not last:
        out_ref[...] = as_codes(
            [
                placed(send_x_ref[...], x_ref[...], coded + 1),
                placed(send_y_ref[...], y_out[...], coded + 1),
            ]
        )


def last_outer_kernel(
    low_ref, high_ref, take_low_ref, take_high_ref, share_ref, part_ref, place_ref, out_ref, a, b, ends
):
    outer_kernel(
        ITERS - 1, True, low_ref, high_ref, take_low_ref, take_high_ref, share_ref, part_ref,
        None, None, None, ends, None, a, b, None, None,
    )
    owned, cells = part_ref.shape
    back = one_hot(place_ref[...], (owned, owned), 1)
    out_ref[:, FACE : cells - FACE] = picked(back, part_ref[:, FACE : cells - FACE])
    out_ref[:, :FACE] = picked(back, ends[:, :FACE])
    out_ref[:, cells - FACE :] = picked(back, ends[:, FACE:])


def on_device(
    resident_now,
    resident_old,
    source_now,
    source_old,
    destination,
    anchor,
    floor_height,
    admit_class,
    admittance,
    neighbours,
):
    members = lax.axis_size("dom")
    slabs = lax.axis_size("slab")
    owned = floor_height.shape[0]
    incoming = anchor.shape[0]
    cells = source_now.shape[1]
    kept = owned - incoming
    f32, bf16, i32 = jnp.float32, jnp.bfloat16, jnp.int32

    slots = source_now.shape[0]
    outgoing = pl.pallas_call(
        functools.partial(pack_kernel, incoming, members),
        out_shape=jax.ShapeDtypeStruct((members, CAP, 2 * cells), bf16),
        grid=(2,),
        in_specs=[pl.BlockSpec(memory_space=pltpu.HBM)] * 3,
        out_specs=pl.BlockSpec((members, CAP, cells), lambda level: (0, 0, level)),
        scratch_shapes=[
            pltpu.VMEM((1, slots), i32),
            pltpu.VMEM((slots, slots), bf16),
            pltpu.VMEM((2, slots, cells), bf16),
            pltpu.SemaphoreType.DMA((3,)),
        ],
        compiler_params=pltpu.CompilerParams(vmem_limit_bytes=60 * 1024 * 1024),
    )(destination[None, :], source_now, source_old)
    got = lax.all_to_all(outgoing, "dom", split_axis=0, concat_axis=0, tiled=True)

    present = neighbours >= 0
    peer_dev = neighbours // owned % members
    peer_slot = neighbours % owned
    slot_ids = jnp.arange(owned, dtype=i32)
    lower = present[5]
    upper = present[4]
    lower_rank = jnp.sum((lower[None, :] & (slot_ids[None, :] < slot_ids[:, None])).astype(i32), axis=1)
    partner_rank = jnp.sum(
        (lower[None, :] & (slot_ids[None, :] < peer_slot[4][:, None])).astype(i32), axis=1
    )
    alone = ~(lower | upper)
    alone_rank = jnp.sum((alone[None, :] & (slot_ids[None, :] < slot_ids[:, None])).astype(i32), axis=1)
    pairs = jnp.sum(lower.astype(i32))
    position = jnp.where(
        lower, 2 * lower_rank, jnp.where(upper, 2 * partner_rank + 1, 2 * pairs + alone_rank)
    )
    order_is = position[None, :] == slot_ids[:, None]
    order = jnp.sum(jnp.where(order_is, slot_ids[None, :], 0), axis=1)
    seat = rank_within(anchor, jnp.arange(incoming, dtype=i32), anchor >= 0)
    inbox = jnp.concatenate([jnp.full((kept,), -1, i32), anchor * CAP + seat])
    class_ids = jnp.arange(admittance.shape[0], dtype=i32)
    send_at = []
    take_at = []
    for d in range(DIRS):
        order_out = rank_within(peer_dev[d], peer_slot[d], present[d])
        order_in = rank_within(peer_dev[d], slot_ids, present[d])
        send_at.append(jnp.where(present[d], peer_dev[d] * ROWS + d % 2 * STEP[d // 2] + order_out, -ROWS))
        take_at.append(jnp.where(present[d], peer_dev[d] * PITCH[d // 2] + (d + 1) % 2 * (d // 2) * CAP + order_in, -ROWS))
    rates = jnp.sum(
        jnp.where(admit_class[:, None] == class_ids[None, :], admittance[None, :], 0.0), axis=1
    )
    near = [present[d].astype(f32) for d in range(6)]
    table = jnp.stack(
        [number.astype(f32) for number in send_at + take_at + [inbox, slot_ids]]
        + [rates, 2.0 * courant_sq / (courant * rates), near[4] + near[5]]
        + near
    )
    table = jnp.sum(jnp.where(order_is[None], table[:, None, :], 0.0), axis=2)
    columns = table[DIRS:].T
    halved = jnp.arange(2, dtype=i32).astype(f32)[None, :] * jnp.array(HALF, f32)[:, None]
    send_at = (table[:DIRS].reshape(2, 1, 2, owned) + halved[:, :, None, None]).reshape(2, -1)
    place = position[:, None].astype(f32)
    heights = floor_height[order].astype(f32)

    grid_shape = jax.ShapeDtypeStruct((owned, cells), f32)
    share = pl.pallas_call(
        prepare_kernel,
        out_shape=grid_shape,
        scratch_shapes=[pltpu.VMEM((owned, cells), f32)],
        compiler_params=VMEM,
    )(heights, columns)
    got, share, columns, send_at, place = lax.optimization_barrier(
        (got, share, columns, send_at, place)
    )

    message = (members, 2 * ROWS, LANES)
    faces_shape = (2 * 2 * owned, LANES)
    faces_scratch = pltpu.VMEM(faces_shape, f32)
    ghost_scratch = pltpu.VMEM((2 * owned, LANES), f32)
    ends_shape = jax.ShapeDtypeStruct((owned, 2 * FACE), f32)
    message_rows = members * ROWS
    *state, outbox = pl.pallas_call(
        begin_kernel,
        out_shape=[grid_shape, ends_shape, jax.ShapeDtypeStruct(message, bf16)],
        scratch_shapes=[faces_scratch, faces_scratch],
        compiler_params=VMEM,
    )(got, resident_now, share, columns, send_at)

    cost = pl.CostEstimate(flops=60 * owned * cells, bytes_accessed=48 * owned * cells, transcendentals=0)
    for sweep in range(ITERS):
        here = lax.all_to_all(outbox, "dom", split_axis=0, concat_axis=0, tiled=True)
        down = lax.slice_in_dim(here, 0, ROWS // 2, axis=1)
        up = lax.slice_in_dim(here, ROWS // 2, ROWS, axis=1)
        from_low = lax.ppermute(up, "slab", [(i, (i + 1) % slabs) for i in range(slabs)])
        from_high = lax.ppermute(down, "slab", [((i + 1) % slabs, i) for i in range(slabs)])
        if sweep == 0:
            part, faces, *lagging, take_y, take_low, take_high, send_x, send_y = (
                pl.pallas_call(
                    first_inner_kernel,
                    out_shape=[grid_shape, jax.ShapeDtypeStruct(faces_shape, f32)]
                    + [grid_shape, ends_shape]
                    + [
                        jax.ShapeDtypeStruct((number * owned, message_rows // share), bf16)
                        for number, share in ((4, 1), (2, 2), (2, 2))
                    ]
                    + [jax.ShapeDtypeStruct((message_rows, 4 * owned), bf16)] * 2,
                    scratch_shapes=[faces_scratch],
                    compiler_params=VMEM,
                    cost_estimate=cost,
                )(here, columns, send_at, got, resident_old, share, *state)
            )
        if sweep:
            fields = (here, take_y, columns, *state, *lagging, share)
        if 0 < sweep < ITERS - 1:
            part, faces = pl.pallas_call(
                functools.partial(inner_kernel, sweep, False),
                out_shape=[grid_shape, jax.ShapeDtypeStruct(faces_shape, f32)],
                scratch_shapes=[faces_scratch],
                compiler_params=VMEM,
                cost_estimate=cost,
            )(*fields)
        if sweep < ITERS - 1:
            edges, outbox = pl.pallas_call(
                functools.partial(outer_kernel, sweep, False),
                out_shape=[ends_shape, jax.ShapeDtypeStruct(message, jnp.int16)],
                scratch_shapes=[ghost_scratch, ghost_scratch, faces_scratch, faces_scratch],
                compiler_params=VMEM,
            )(from_low, from_high, take_low, take_high, share, part, faces, send_x, send_y)
        else:
            part = pl.pallas_call(
                last_inner_kernel,
                out_shape=grid_shape,
                scratch_shapes=[faces_scratch],
                compiler_params=VMEM,
                cost_estimate=cost,
            )(*fields)
            return pl.pallas_call(
                last_outer_kernel,
                out_shape=grid_shape,
                scratch_shapes=[ghost_scratch, ghost_scratch, pltpu.VMEM((owned, 2 * FACE), f32)],
                compiler_params=VMEM,
            )(from_low, from_high, take_low, take_high, share, part, place)
        lagging, state = state, (part, edges)


def solution(mesh):
    split = P(("slab", "dom"), None)
    line = P(("slab", "dom"))
    return jax.shard_map(
        on_device,
        mesh=mesh,
        in_specs=(split, split, split, split, line, line, split, line, P(), P(None, ("slab", "dom"))),
        out_specs=split,
        check_vma=False,
    )
```

```python
import functools
import math

import jax
import jax.numpy as jnp
from jax import lax
from jax.experimental import pallas as pl
from jax.experimental.pallas import tpu as pltpu
from jax.sharding import PartitionSpec as P

EDGE = 16
CAP = 2
ITERS = 4
FACE = EDGE * EDGE
CELLS = EDGE * FACE
LANES = 128
SUB = 8
DIRS = 4
ROWS = DIRS * CAP

STEP = (2 * CAP, CAP)
HALF = (CAP, 2 * CAP)
PITCH = (ROWS // 2, ROWS)

TAKE, INBOX, RATE, WEIGHT, JOINED, NEAR = 0, 4, 5, 6, 7, 8

courant_sq = 0.3
courant = 0.3**0.5

OCTAVE = 1024.0


def lowest(steps):
    return 32767.0 / OCTAVE - 0.01 - math.log2(6.0 * 3.0**steps)

VMEM = pltpu.CompilerParams(vmem_limit_bytes=16 * 1024 * 1024)


def rank_within(groups, orderings, usable):
    earlier = (
        (groups[:, None] == groups[None, :])
        & (orderings[None, :] < orderings[:, None])
        & usable[None, :]
    )
    return jnp.sum(earlier.astype(jnp.int32), axis=1)


def encode(values, low):
    size = jnp.abs(values)
    level = jnp.floor((jnp.log2(jnp.maximum(size, 1e-30)) + low) * OCTAVE + 0.5)
    level = jnp.clip(level, 0.0, 32767.0)
    return jnp.where(values < 0.0, -level, level)


def decode(level, low):
    size = jnp.exp2(jnp.abs(level) * (1.0 / OCTAVE) - low)
    return jnp.where(level > 0.0, size, jnp.where(level < 0.0, -size, 0.0))


def picked(matrix, values):
    high = values.astype(jnp.bfloat16)
    low = (values - high.astype(jnp.float32)).astype(jnp.bfloat16)
    width = values.shape[1]
    if width == LANES:
        both = jnp.dot(
            matrix, jnp.concatenate([high, low], axis=1), preferred_element_type=jnp.float32
        )
        return both[:, :width] + both[:, width:]
    return jnp.dot(matrix, high, preferred_element_type=jnp.float32) + jnp.dot(
        matrix, low, preferred_element_type=jnp.float32
    )


def turn(block, shift, axis=1):
    size = block.shape[axis]
    shift = shift % size
    return pltpu.roll(block, shift, axis) if shift else block


class Grid:
    def __init__(self, joined):
        lane = lax.broadcasted_iota(jnp.int32, (SUB, LANES), 1)
        row = lax.broadcasted_iota(jnp.int32, (SUB, LANES), 0)
        self.first_y = lane < EDGE
        self.last_y = lane >= LANES - EDGE
        self.bottom = lane % EDGE == 0
        self.top = lane % EDGE == EDGE - 1
        self.odd = row % 2 == 1
        self.strip = lane // EDGE
        upper = jnp.where(self.odd, 1.0, 0.0)
        self.partner = joined * jnp.where(
            self.bottom, upper, jnp.where(self.top, 1.0 - upper, 0.0)
        )

    def along_z(self, block):
        given = jnp.where(self.odd, turn(block, EDGE - 1), turn(block, 1 - EDGE))
        across = jnp.where(self.odd, turn(given, 1, 0), turn(given, -1, 0))
        below = jnp.where(self.bottom, 0.0, turn(block, 1))
        above = jnp.where(self.top, 0.0, turn(block, -1))
        return (below + above) + across * self.partner

    def total(self, plane, x, ghost_x, ghost_y):
        first, second = plane(x)
        sides = [plane(at) for at in (x - 1, x + 1) if 0 <= at < EDGE]
        if ghost_x is not None and x in (0, EDGE - 1):
            sides.append(ghost_x(x))
        along_x = [sum(side[half] for side in sides) for half in range(2)]
        up_first, up_second = turn(first, EDGE), turn(second, EDGE)
        down_first, down_second = turn(first, -EDGE), turn(second, -EDGE)
        low, high = ghost_y(x)
        total_first = (
            along_x[0]
            + (jnp.where(self.first_y, low, up_first) + jnp.where(self.last_y, down_second, down_first))
            + self.along_z(first)
        )
        total_second = (
            along_x[1]
            + (jnp.where(self.first_y, up_first, up_second) + jnp.where(self.last_y, high, down_second))
            + self.along_z(second)
        )
        return total_first, total_second


def pieces(ref, rows, x):
    at = x * FACE
    return ref[rows, at : at + LANES], ref[rows, at + LANES : at + FACE]


def plane(ref, ends_ref, rows, x):
    if x in (0, EDGE - 1):
        return pieces(ends_ref, rows, 1 if x else 0)
    return pieces(ref, rows, x)


def at_rows(base, group):
    return pl.ds(pl.multiple_of(base + group * SUB, SUB), SUB)


def pack_faces_x(ref, owned, group, x, first, second):
    direction = 1 if x else 0
    ref[at_rows(direction * owned, group), :] = first
    ref[at_rows((2 + direction) * owned, group), :] = second


def pack_faces_y(ref, owned, grid, state_ref, group):
    rows = at_rows(0, group)
    for half in range(2):
        low, high = None, None
        for place in range(SUB):
            first, second = pieces(state_ref, rows, half * SUB + place)
            here = grid.strip == place
            first, second = turn(first, EDGE * place), turn(second, EDGE * (place + 1))
            low = first if place == 0 else jnp.where(here, first, low)
            high = second if place == 0 else jnp.where(here, second, high)
        ref[at_rows(2 * half * owned, group), :] = low
        ref[at_rows((2 * half + 1) * owned, group), :] = high


def one_hot(numbers, shape, axis):
    at = lax.broadcasted_iota(jnp.int32, shape, axis).astype(jnp.float32)
    return jnp.where(numbers == at, 1.0, 0.0).astype(jnp.bfloat16)


def placed(matrix, faces, coded):
    if coded:
        rows = picked(matrix, encode(faces, lowest(coded)))
    else:
        rows = jnp.dot(
            matrix, faces.astype(jnp.bfloat16), preferred_element_type=jnp.float32
        )
    return rows.reshape(rows.shape[0] // ROWS, ROWS, LANES)


def taken(matrix, message, coded, first=0):
    if coded:
        message = message.astype(jnp.int32)
    message = message.astype(jnp.float32)[:, first:, :]
    message = message.reshape(message.shape[0] * message.shape[1], LANES)
    if coded:
        return decode(picked(matrix, message), lowest(coded))
    return jnp.dot(matrix, message.astype(jnp.bfloat16), preferred_element_type=jnp.float32)


def as_codes(parts):
    return jnp.concatenate(parts, axis=1).astype(jnp.int32).astype(jnp.int16)


def groups(owned, body):
    def step(group, carry):
        body(group)
        return carry

    lax.fori_loop(0, owned // SUB, step, 0)


def pack_kernel(
    incoming, members, dest_hbm, now_hbm, old_hbm, out_ref, dest_ref, chosen_ref, held, arrived
):
    level = pl.program_id(0)
    slots = dest_ref.shape[1]
    copies = [
        pltpu.make_async_copy(now_hbm, held.at[0], arrived.at[0]),
        pltpu.make_async_copy(old_hbm, held.at[1], arrived.at[1]),
    ]

    @pl.when(level == 0)
    def _():
        first = pltpu.make_async_copy(dest_hbm, dest_ref, arrived.at[2])
        first.start()
        for copy in copies:
            copy.start()
        first.wait()
        dest = dest_ref[...]
        src = lax.broadcasted_iota(jnp.int32, (slots, slots), 1)
        other = lax.broadcasted_iota(jnp.int32, (slots, slots), 0)
        across = jnp.broadcast_to(dest, (slots, slots))
        down = jnp.sum(jnp.where(src == other, across, 0), axis=1, keepdims=True)
        receiver = jnp.zeros((1, slots), jnp.int32)
        for member in range(1, members):
            receiver = receiver + (dest >= member * incoming).astype(jnp.int32)
        earlier = (down >= receiver * incoming) & (down < dest)
        place = jnp.sum(earlier.astype(jnp.int32), axis=0, keepdims=True)
        spot = jnp.where(dest >= 0, receiver * CAP + place, -1)
        chosen_ref[...] = jnp.where(other == spot, 1.0, 0.0).astype(jnp.bfloat16)
        copies[0].wait()

    @pl.when(level == 1)
    def _():
        copies[1].wait()

    rows = jnp.dot(chosen_ref[...], held[level], preferred_element_type=jnp.float32)
    out_ref[...] = rows.astype(jnp.bfloat16).reshape(out_ref.shape)


def prepare_kernel(height_ref, column_ref, share_ref, mask_ref):
    owned = height_ref.shape[0]
    row = lax.broadcasted_iota(jnp.int32, (FACE, FACE), 0)
    column = lax.broadcasted_iota(jnp.int32, (FACE, FACE), 1)
    level = (lax.broadcasted_iota(jnp.int32, (owned, FACE), 1) % EDGE).astype(jnp.float32)
    heights = height_ref[...].astype(jnp.bfloat16)
    for x in range(EDGE):
        spread = jnp.where(row == column // EDGE + x * EDGE, 1.0, 0.0).astype(jnp.bfloat16)
        floor = jnp.dot(heights, spread, preferred_element_type=jnp.float32)
        mask_ref[:, x * FACE : (x + 1) * FACE] = jnp.where(level >= floor, 1.0, 0.0)

    def count(group):
        rows = at_rows(0, group)
        columns = column_ref[rows, :]
        near = [
            jnp.broadcast_to(columns[:, at : at + 1], (SUB, LANES))
            for at in range(NEAR, NEAR + 6)
        ]
        rate = jnp.broadcast_to(columns[:, RATE : RATE + 1], (SUB, LANES))
        grid = Grid(near[4] + near[5])
        for x in range(EDGE):
            total = grid.total(
                lambda at: pieces(mask_ref, rows, at),
                x,
                lambda at: (near[1], near[1]) if at else (near[0], near[0]),
                lambda at: (near[2], near[3]),
            )
            air = pieces(mask_ref, rows, x)
            for half in range(2):
                at = slice(x * FACE + half * LANES, x * FACE + (half + 1) * LANES)
                damping = courant * (6.0 - total[half]) * rate / 2.0
                share_ref[rows, at] = air[half] / (1.0 + damping)

    groups(owned, count)


def settled(got_ref, own_ref, columns, index, to_ref, ends_ref, share_ref):
    owned, cells = to_ref.shape
    members = got_ref.shape[0]
    arrived = got_ref[:, :, index * cells : (index + 1) * cells].reshape(members * CAP, cells)
    bricks = jnp.concatenate([arrived, own_ref[...]], axis=0)
    chosen = one_hot(columns[:, INBOX : INBOX + 1], (owned, bricks.shape[0]), 1)
    rows = jnp.dot(chosen, bricks, preferred_element_type=jnp.float32)
    to_ref[...] = jnp.where(share_ref[...] > 0.0, rows, 0.0)
    ends_ref[:, :FACE] = to_ref[:, :FACE]
    ends_ref[:, FACE:] = to_ref[:, cells - FACE :]


def begin_kernel(
    got_ref, own_ref, share_ref, column_ref, send_at_ref, p_ref, ends_ref, out_ref, x_ref, y_ref
):
    members = got_ref.shape[0]
    owned = p_ref.shape[0]
    settled(got_ref, own_ref, column_ref[...], 0, p_ref, ends_ref, share_ref)
    grid = Grid(jnp.ones((SUB, LANES), jnp.float32))

    def faces(group):
        for x in (0, EDGE - 1):
            pack_faces_x(x_ref, owned, group, x, *pieces(p_ref, at_rows(0, group), x))
        pack_faces_y(y_ref, owned, grid, p_ref, group)

    groups(owned, faces)
    shape = (members * ROWS, 4 * owned)
    parts = [
        placed(one_hot(send_at_ref[index : index + 1, :], shape, 0), ref[...], 0)
        for index, ref in enumerate((x_ref, y_ref))
    ]
    out_ref[...] = jnp.concatenate(parts, axis=1).astype(jnp.bfloat16)


def inner_kernel(
    coded,
    last,
    here_ref,
    take_ref,
    column_ref,
    p_ref,
    p_ends_ref,
    q_ref,
    q_ends_ref,
    share_ref,
    new_ref,
    y_ref,
    ghost_ref,
):
    owned = p_ref.shape[0]
    ghost_ref[...] = taken(take_ref[...], here_ref[...], coded, ROWS)

    def advance(group):
        rows = at_rows(0, group)
        grid = Grid(jnp.broadcast_to(column_ref[rows, JOINED : JOINED + 1], (SUB, LANES)))
        weight = jnp.broadcast_to(column_ref[rows, WEIGHT : WEIGHT + 1], (SUB, LANES))
        inward = (2.0 - 6.0 * courant_sq) - weight
        low, high = (
            [ghost_ref[at_rows((2 * half + d) * owned, group), :] for half in range(2)]
            for d in range(2)
        )

        def ghost_y(x):
            half, place = x // SUB, x % SUB
            return turn(low[half], -EDGE * place), turn(high[half], -EDGE * (place + 1))

        for x in range(EDGE):
            total = grid.total(lambda at: plane(p_ref, p_ends_ref, rows, at), x, None, ghost_y)
            state = plane(p_ref, p_ends_ref, rows, x)
            lagging = plane(q_ref, q_ends_ref, rows, x)
            share = pieces(share_ref, rows, x)
            for h in range(2):
                new_ref[rows, x * FACE + h * LANES : x * FACE + (h + 1) * LANES] = share[h] * (
                    inward * state[h] + courant_sq * total[h] - 2.0 * lagging[h]
                ) + (lagging[h] + weight * state[h])

    groups(owned, advance)
    if not last:
        grid = Grid(jnp.ones((SUB, LANES), jnp.float32))
        groups(owned, lambda group: pack_faces_y(y_ref, owned, grid, new_ref, group))


def first_inner_kernel(
    here_ref,
    column_ref,
    send_at_ref,
    got_ref,
    own_ref,
    share_ref,
    p_ref,
    p_ends_ref,
    part_ref,
    y_ref,
    q_ref,
    q_ends_ref,
    take_y_ref,
    take_low_ref,
    take_high_ref,
    send_x_ref,
    send_y_ref,
    ghost_ref,
):
    owned = p_ref.shape[0]
    columns = column_ref[...]
    settled(got_ref, own_ref, columns, 1, q_ref, q_ends_ref, share_ref)
    for ref, directions in ((take_y_ref, (2, 3)), (take_low_ref, (0,)), (take_high_ref, (1,))):
        numbers = [
            columns[:, TAKE + d : TAKE + d + 1] + HALF[d // 2] * half
            for half in range(2)
            for d in directions
        ]
        ref[...] = one_hot(jnp.concatenate(numbers, axis=0), ref.shape, 1)
    for index, ref in enumerate((send_x_ref, send_y_ref)):
        ref[...] = one_hot(send_at_ref[index : index + 1, :], ref.shape, 0)

    inner_kernel(
        0, False, here_ref, take_y_ref, column_ref, p_ref, p_ends_ref, q_ref, q_ends_ref,
        share_ref, part_ref, y_ref, ghost_ref,
    )


def last_inner_kernel(*refs):
    *ins, place_ref, middle_ref, ends_ref, part_ref, ghost_ref = refs
    inner_kernel(ITERS - 1, True, *ins, part_ref, None, ghost_ref)
    owned, cells = part_ref.shape
    back = one_hot(place_ref[...], (owned, owned), 1)
    middle_ref[...] = picked(back, part_ref[:, FACE : cells - FACE])
    ends_ref[:, :FACE] = part_ref[:, :FACE]
    ends_ref[:, FACE:] = part_ref[:, cells - FACE :]


def outer_kernel(
    coded,
    last,
    low_ref,
    high_ref,
    take_low_ref,
    take_high_ref,
    share_ref,
    part_ref,
    y_ref,
    send_x_ref,
    send_y_ref,
    ends_ref,
    out_ref,
    ghost_low,
    ghost_high,
    x_ref,
    y_out,
):
    owned = part_ref.shape[0]
    ghost_low[...] = taken(take_low_ref[...], low_ref[...], coded)
    ghost_high[...] = taken(take_high_ref[...], high_ref[...], coded)
    grid = Grid(jnp.ones((SUB, LANES), jnp.float32))
    if not last:
        y_out[...] = y_ref[...]

    def finish(group):
        rows = at_rows(0, group)
        for x, ghost in ((0, ghost_low), (EDGE - 1, ghost_high)):
            part = pieces(part_ref, rows, int(x > 0) if last else x)
            share = pieces(share_ref, rows, x)
            done = [
                part[h] + courant_sq * share[h] * ghost[at_rows(h * owned, group), :] for h in range(2)
            ]
            for h in range(2):
                at = (FACE if x else 0) + h * LANES
                ends_ref[rows, at : at + LANES] = done[h]
            if last:
                continue
            pack_faces_x(x_ref, owned, group, x, *done)
            half, place = x // SUB, x % SUB
            here = grid.strip == place
            for d, face in enumerate(
                (turn(done[0], EDGE * place), turn(done[1], EDGE * (place + 1)))
            ):
                at = at_rows((2 * half + d) * owned, group)
                y_out[at, :] = jnp.where(here, face, y_out[at, :])

    groups(owned, finish)
    if not last:
        out_ref[...] = as_codes(
            [
                placed(send_x_ref[...], x_ref[...], coded + 1),
                placed(send_y_ref[...], y_out[...], coded + 1),
            ]
        )


def last_outer_kernel(
    low_ref, high_ref, take_low_ref, take_high_ref, share_ref, part_ref, middle_ref, place_ref, out_ref, a, b, ends
):
    outer_kernel(
        ITERS - 1, True, low_ref, high_ref, take_low_ref, take_high_ref, share_ref, part_ref,
        None, None, None, ends, None, a, b, None, None,
    )
    owned, cells = out_ref.shape
    back = one_hot(place_ref[...], (owned, owned), 1)
    out_ref[:, FACE : cells - FACE] = middle_ref[...]
    out_ref[:, :FACE] = picked(back, ends[:, :FACE])
    out_ref[:, cells - FACE :] = picked(back, ends[:, FACE:])


def on_device(
    resident_now,
    resident_old,
    source_now,
    source_old,
    destination,
    anchor,
    floor_height,
    admit_class,
    admittance,
    neighbours,
):
    members = lax.axis_size("dom")
    slabs = lax.axis_size("slab")
    owned = floor_height.shape[0]
    incoming = anchor.shape[0]
    cells = source_now.shape[1]
    kept = owned - incoming
    f32, bf16, i32 = jnp.float32, jnp.bfloat16, jnp.int32

    slots = source_now.shape[0]
    outgoing = pl.pallas_call(
        functools.partial(pack_kernel, incoming, members),
        out_shape=jax.ShapeDtypeStruct((members, CAP, 2 * cells), bf16),
        grid=(2,),
        in_specs=[pl.BlockSpec(memory_space=pltpu.HBM)] * 3,
        out_specs=pl.BlockSpec((members, CAP, cells), lambda level: (0, 0, level)),
        scratch_shapes=[
            pltpu.VMEM((1, slots), i32),
            pltpu.VMEM((slots, slots), bf16),
            pltpu.VMEM((2, slots, cells), bf16),
            pltpu.SemaphoreType.DMA((3,)),
        ],
        compiler_params=pltpu.CompilerParams(vmem_limit_bytes=60 * 1024 * 1024),
    )(destination[None, :], source_now, source_old)
    got = lax.all_to_all(outgoing, "dom", split_axis=0, concat_axis=0, tiled=True)

    present = neighbours >= 0
    peer_dev = neighbours // owned % members
    peer_slot = neighbours % owned
    slot_ids = jnp.arange(owned, dtype=i32)
    lower = present[5]
    upper = present[4]
    lower_rank = jnp.sum((lower[None, :] & (slot_ids[None, :] < slot_ids[:, None])).astype(i32), axis=1)
    partner_rank = jnp.sum(
        (lower[None, :] & (slot_ids[None, :] < peer_slot[4][:, None])).astype(i32), axis=1
    )
    alone = ~(lower | upper)
    alone_rank = jnp.sum((alone[None, :] & (slot_ids[None, :] < slot_ids[:, None])).astype(i32), axis=1)
    pairs = jnp.sum(lower.astype(i32))
    position = jnp.where(
        lower, 2 * lower_rank, jnp.where(upper, 2 * partner_rank + 1, 2 * pairs + alone_rank)
    )
    order_is = position[None, :] == slot_ids[:, None]
    order = jnp.sum(jnp.where(order_is, slot_ids[None, :], 0), axis=1)
    seat = rank_within(anchor, jnp.arange(incoming, dtype=i32), anchor >= 0)
    inbox = jnp.concatenate([members * CAP + jnp.arange(kept, dtype=i32), anchor * CAP + seat])
    class_ids = jnp.arange(admittance.shape[0], dtype=i32)
    send_at = []
    take_at = []
    for d in range(DIRS):
        order_out = rank_within(peer_dev[d], peer_slot[d], present[d])
        order_in = rank_within(peer_dev[d], slot_ids, present[d])
        send_at.append(jnp.where(present[d], peer_dev[d] * ROWS + d % 2 * STEP[d // 2] + order_out, -ROWS))
        take_at.append(jnp.where(present[d], peer_dev[d] * PITCH[d // 2] + (d + 1) % 2 * (d // 2) * CAP + order_in, -ROWS))
    rates = jnp.sum(
        jnp.where(admit_class[:, None] == class_ids[None, :], admittance[None, :], 0.0), axis=1
    )
    near = [present[d].astype(f32) for d in range(6)]
    table = jnp.stack(
        [number.astype(f32) for number in send_at + take_at + [inbox]]
        + [rates, 2.0 * courant_sq / (courant * rates), near[4] + near[5]]
        + near
    )
    table = jnp.sum(jnp.where(order_is[None], table[:, None, :], 0.0), axis=2)
    columns = table[DIRS:].T
    halved = jnp.arange(2, dtype=i32).astype(f32)[None, :] * jnp.array(HALF, f32)[:, None]
    send_at = (table[:DIRS].reshape(2, 1, 2, owned) + halved[:, :, None, None]).reshape(2, -1)
    place = position[:, None].astype(f32)
    heights = floor_height[order].astype(f32)

    grid_shape = jax.ShapeDtypeStruct((owned, cells), f32)
    share = pl.pallas_call(
        prepare_kernel,
        out_shape=grid_shape,
        scratch_shapes=[pltpu.VMEM((owned, cells), f32)],
        compiler_params=VMEM,
    )(heights, columns)
    got, share, columns, send_at, place = lax.optimization_barrier(
        (got, share, columns, send_at, place)
    )

    message = (members, 2 * ROWS, LANES)
    faces_shape = (2 * 2 * owned, LANES)
    faces_scratch = pltpu.VMEM(faces_shape, f32)
    ghost_scratch = pltpu.VMEM((2 * owned, LANES), f32)
    ends_shape = jax.ShapeDtypeStruct((owned, 2 * FACE), f32)
    message_rows = members * ROWS
    *state, outbox = pl.pallas_call(
        begin_kernel,
        out_shape=[grid_shape, ends_shape, jax.ShapeDtypeStruct(message, bf16)],
        scratch_shapes=[faces_scratch, faces_scratch],
        compiler_params=VMEM,
    )(got, resident_now, share, columns, send_at)

    cost = pl.CostEstimate(flops=60 * owned * cells, bytes_accessed=48 * owned * cells, transcendentals=0)
    for sweep in range(ITERS):
        here = lax.all_to_all(outbox, "dom", split_axis=0, concat_axis=0, tiled=True)
        down = lax.slice_in_dim(here, 0, ROWS // 2, axis=1)
        up = lax.slice_in_dim(here, ROWS // 2, ROWS, axis=1)
        from_low = lax.ppermute(up, "slab", [(i, (i + 1) % slabs) for i in range(slabs)])
        from_high = lax.ppermute(down, "slab", [((i + 1) % slabs, i) for i in range(slabs)])
        if sweep == 0:
            part, faces, *lagging, take_y, take_low, take_high, send_x, send_y = (
                pl.pallas_call(
                    first_inner_kernel,
                    out_shape=[grid_shape, jax.ShapeDtypeStruct(faces_shape, f32)]
                    + [grid_shape, ends_shape]
                    + [
                        jax.ShapeDtypeStruct((number * owned, message_rows // share), bf16)
                        for number, share in ((4, 1), (2, 2), (2, 2))
                    ]
                    + [jax.ShapeDtypeStruct((message_rows, 4 * owned), bf16)] * 2,
                    scratch_shapes=[faces_scratch],
                    compiler_params=VMEM,
                    cost_estimate=cost,
                )(here, columns, send_at, got, resident_old, share, *state)
            )
        if sweep:
            fields = (here, take_y, columns, *state, *lagging, share)
        if 0 < sweep < ITERS - 1:
            part, faces = pl.pallas_call(
                functools.partial(inner_kernel, sweep, False),
                out_shape=[grid_shape, jax.ShapeDtypeStruct(faces_shape, f32)],
                scratch_shapes=[faces_scratch],
                compiler_params=VMEM,
                cost_estimate=cost,
            )(*fields)
        if sweep < ITERS - 1:
            edges, outbox = pl.pallas_call(
                functools.partial(outer_kernel, sweep, False),
                out_shape=[ends_shape, jax.ShapeDtypeStruct(message, jnp.int16)],
                scratch_shapes=[ghost_scratch, ghost_scratch, faces_scratch, faces_scratch],
                compiler_params=VMEM,
            )(from_low, from_high, take_low, take_high, share, part, faces, send_x, send_y)
        else:
            middle, part = pl.pallas_call(
                last_inner_kernel,
                out_shape=[jax.ShapeDtypeStruct((owned, cells - 2 * FACE), f32), ends_shape],
                scratch_shapes=[pltpu.VMEM((owned, cells), f32), faces_scratch],
                compiler_params=VMEM,
                cost_estimate=cost,
            )(*fields, place)
            return pl.pallas_call(
                last_outer_kernel,
                out_shape=grid_shape,
                scratch_shapes=[ghost_scratch, ghost_scratch, pltpu.VMEM((owned, 2 * FACE), f32)],
                compiler_params=VMEM,
            )(from_low, from_high, take_low, take_high, share, part, middle, place)
        lagging, state = state, (part, edges)


def solution(mesh):
    split = P(("slab", "dom"), None)
    line = P(("slab", "dom"))
    return jax.shard_map(
        on_device,
        mesh=mesh,
        in_specs=(split, split, split, split, line, line, split, line, P(), P(None, ("slab", "dom"))),
        out_specs=split,
        check_vma=False,
    )
```
